32 devices in a mesh: grp: 2 (over x), sx: 16 (over z, y, core).
Axes of the slice: x: 2, y: 2, z: 4, core: 2. Of those that a mesh axis runs over, the one named last changes fastest.
Arguments:
- right_side: float32 [128, 256, 128], P(('grp', 'sx')), parts along dimension 0, may hold values from -6 to 6
- storage: float32 [128, 256, 128], P(('grp', 'sx')), parts along dimension 0, may hold values from 0.05 to 0.5
- trans_x: float32 [512, 128], P('grp'), parts along dimension 0, may hold values from 0.1 to 1
- trans_y: float32 [128, 256, 128], P(('grp', 'sx')), parts along dimension 0, may hold values from 0.1 to 1
- trans_z: float32 [128, 256, 128], P(('grp', 'sx')), parts along dimension 0, may hold values from 0.1 to 1
- well_cells: int32 [32], P('grp'), parts along dimension 0, may hold values from 0 to 2097151
- well_rates: float32 [32], P('grp'), parts along dimension 0, may hold values from -40 to 40
- sat_logit: float32 [128, 256, 128], P(('grp', 'sx')), parts along dimension 0, may hold values from -8 to 8
- porosity: float32 [128, 256, 128], P(('grp', 'sx')), parts along dimension 0, may hold values from 0.1 to 0.3
- y_index: int32 [128], replicated, may hold values from -1 to 62, as said below
- y_frac: float32 [128], replicated, may hold values from 0 to 1
- z_index: int32 [256], replicated, may hold values from -1 to 126, as said below
- z_frac: float32 [256], replicated, may hold values from 0 to 1
- background: float32 [128, 512, 256], P(None, ('grp', 'sx')), parts along dimension 1, may hold values from 0.55 to 0.85
- wave_prev: float32 [128, 512, 256], P(None, ('grp', 'sx')), parts along dimension 1, may hold values from -6 to 6
- wave_now: float32 [128, 512, 256], P(None, ('grp', 'sx')), parts along dimension 1, may hold values from -6 to 6
- data_residual: float32 [128, 512, 256], P(None, ('grp', 'sx')), parts along dimension 1, may hold values from -6 to 6
Outputs:
- pressure: float32 [128, 256, 128], P(('grp', 'sx')), parts along dimension 0
- wavefield: float32 [128, 512, 256], P(None, ('grp', 'sx')), parts along dimension 1
- sat_gradient: float32 [128, 256, 128], P(('grp', 'sx')), parts along dimension 0
The draws below stay inside these ranges and needn't reach their ends.
There are 2 independent parts, one for each index of `grp`. The reference program is written for one: setup_inputs(seed, part) draws one part's arguments, and reference() takes and returns one part's arrays. A program takes and returns all parts, laid end to end along the dimension named above; an argument that names none is the same for every part. Nothing has to cross between parts.
Inputs may be any that keep to these rules, and one draw needn't show every extreme that they name: -1 marks a seismic row outside the reservoir; otherwise cells y_index and y_index + 1 along i are blended. -1 marks a depth outside the reservoir; otherwise layers z_index and z_index + 1 are blended. `well_cells`: flat index (i * 256 + j) * 128 + k; a cell may hold several wells.
All inputs are finite; a program needn't handle non-finite values.
Results may differ from the reference program's by a relative error of at most 0.0003.
Values sent between devices are 32-bit elements; how exact they have to be, the bound alone decides.
A program may use at most 128 MiB of HBM per device.

```python
import math
import jax
import jax.numpy as jnp
from jax import lax

FZ = 128
SY = 128
SZ = 256
ITERS = 2
STEPS = 4
WELLS = 16
NI = 64
FY = 256
NXS = 256


def draw_y_index(key, part):
    key = jax.random.fold_in(key, 11)
    values = jax.random.randint(key, (SY,), -1, NI - 1)
    return values.at[0].set(-1).at[1].set(NI - 2)


def draw_z_index(key, part):
    key = jax.random.fold_in(key, 23)
    values = jax.random.randint(key, (SZ,), -1, FZ - 1)
    return values.at[0].set(-1).at[1].set(FZ - 2)


def place_ends(values, rng, low, top_value):
    shape = values.shape
    spot = [jax.random.randint(jax.random.fold_in(rng, axis), (), 0, shape[axis]) for axis in range(len(shape))]
    values = values.at[tuple(spot)].set(low)
    longest = shape.index(max(shape))
    spot[longest] = (spot[longest] + 1) % shape[longest]
    return values.at[tuple(spot)].set(top_value)


def level_of(stream_key, shape, pieces, smallest, top_value):
    factor_of, own = 1.0, jax.random.fold_in(stream_key, 6)
    for axis_at, parts in pieces:
        steps = jnp.exp(jax.random.uniform(jax.random.fold_in(own, axis_at), (parts,), jnp.float32, smallest / len(pieces), top_value / len(pieces)))
        factor_of = factor_of * jnp.repeat(steps, shape[axis_at] // parts).reshape([-1 if axis == axis_at else 1 for axis in range(len(shape))])
    return factor_of


def centred(stream_key, shape, spread, most, shards=(), kind=jnp.bfloat16):
    drawn = jax.random.normal(stream_key, shape, jnp.float32) * spread
    if len(shards) > 0:
        drawn = level_of(stream_key, shape, shards, -0.22, 0.18) * drawn
    return jnp.clip(drawn, min=-most, max=most).astype(kind)


def setup_inputs(seed: int = 0, part: int = 0) -> dict:
    splits = jax.random.split(jax.random.key(seed), 18)
    part_splits = jax.random.split(jax.random.fold_in(splits[17], part), 18)
    right_side = centred(part_splits[0], (NI, FY, FZ), 1.0, 6.0, ((0, 16),), jnp.float32)
    storage = jnp.clip(jnp.exp(math.log(0.5) - 2.3025851 * jax.random.uniform(part_splits[1], (NI, FY, FZ), jnp.float32) ** level_of(part_splits[1], (NI, FY, FZ), ((0, 16),), -0.2, 0.2)), 0.05, 0.5)
    trans_x = jnp.clip(jnp.exp(jax.random.uniform(part_splits[2], (FY, FZ), jnp.float32, math.log(0.1), math.log(1.0))), 0.1, 1.0)
    trans_y = jnp.clip(jnp.exp(math.log(1.0) - 2.3025851 * jax.random.uniform(part_splits[3], (NI, FY, FZ), jnp.float32) ** level_of(part_splits[3], (NI, FY, FZ), ((0, 16),), -0.2, 0.2)), 0.1, 1.0)
    trans_z = jnp.clip(jnp.exp(math.log(1.0) - 2.3025851 * jax.random.uniform(part_splits[4], (NI, FY, FZ), jnp.float32) ** level_of(part_splits[4], (NI, FY, FZ), ((0, 16),), -0.2, 0.2)), 0.1, 1.0)
    well_cells = place_ends(jax.random.randint(part_splits[5], (WELLS,), 0, NI * FY * FZ), jax.random.fold_in(part_splits[5], 1), 0, (NI * FY * FZ) - 1).astype(jnp.int32)
    well_rates = centred(part_splits[6], (WELLS,), 10.0, 40.0, (), jnp.float32)
    sat_logit = centred(part_splits[7], (NI, FY, FZ), 1.5, 8.0, ((0, 16),), jnp.float32)
    porosity = jnp.clip(0.1 + 0.20000001043081284 * jax.random.uniform(part_splits[8], (NI, FY, FZ), jnp.float32) ** level_of(part_splits[8], (NI, FY, FZ), ((0, 16),), -0.2, 0.2), 0.1, 0.3)
    y_index = draw_y_index(jax.random.fold_in(splits[17], 71), part)
    y_frac = jnp.clip(jax.random.uniform(splits[10], (SY,), jnp.float32, 0.0, 1.0), 0.0, 1.0)
    z_index = draw_z_index(jax.random.fold_in(splits[17], 71), part)
    z_frac = jnp.clip(jax.random.uniform(splits[12], (SZ,), jnp.float32, 0.0, 1.0), 0.0, 1.0)
    background = jnp.clip(0.55 + 0.3 * jax.random.uniform(part_splits[13], (SY, NXS, SZ), jnp.float32) ** level_of(part_splits[13], (SY, NXS, SZ), ((1, 16),), -0.2, 0.2), 0.55, 0.85)
    wave_prev = centred(part_splits[14], (SY, NXS, SZ), 1.0, 6.0, ((1, 16),), jnp.float32)
    wave_now = centred(part_splits[15], (SY, NXS, SZ), 1.0, 6.0, ((1, 16),), jnp.float32)
    data_residual = centred(part_splits[16], (SY, NXS, SZ), 1.0, 6.0, ((1, 16),), jnp.float32)
    return {"right_side": right_side, "storage": storage, "trans_x": trans_x, "trans_y": trans_y, "trans_z": trans_z, "well_cells": well_cells, "well_rates": well_rates, "sat_logit": sat_logit, "porosity": porosity, "y_index": y_index, "y_frac": y_frac, "z_index": z_index, "z_frac": z_frac, "background": background, "wave_prev": wave_prev, "wave_now": wave_now, "data_residual": data_residual}


courant = 0.25
transport = 2.0
velocity_ref = 22.5
mineral_bulk = 37.0
mineral_shear = 44.0
carbon_bulk = 0.08
brine_bulk = 2.5
mineral_density = 2.65
carbon_density = 0.7
brine_density = 1.03

def lateral(values, trans_y, trans_z):
    upper_y = jnp.pad(values[:, 1:], ((0, 0), (0, 1), (0, 0)))
    lower_y = jnp.pad(values[:, :-1], ((0, 0), (1, 0), (0, 0)))
    below_y = jnp.pad(trans_y[:, :-1], ((0, 0), (1, 0), (0, 0)))
    upper_z = jnp.pad(values[:, :, 1:], ((0, 0), (0, 0), (0, 1)))
    lower_z = jnp.pad(values[:, :, :-1], ((0, 0), (0, 0), (1, 0)))
    below_z = jnp.pad(trans_z[:, :, :-1], ((0, 0), (0, 0), (1, 0)))
    return trans_y * (values - upper_y) + below_y * (values - lower_y) + trans_z * (values - upper_z) + below_z * (values - lower_z)

def flow_apply(values, storage, trans_x, trans_y, trans_z):
    padded = jnp.pad(values, ((1, 1), (0, 0), (0, 0)))
    along_i = trans_x[None] * (2.0 * values - padded[2:] - padded[:-2])
    return storage * values + along_i + lateral(values, trans_y, trans_z)

def perturb(saturation, porosity):
    fluid_bulk = 1.0 / (saturation / carbon_bulk + (1.0 - saturation) / brine_bulk)
    frame_factor = (1.0 - porosity) ** 3
    dry_bulk = mineral_bulk * frame_factor
    shear_mod = mineral_shear * frame_factor
    biot_ratio = 1.0 - dry_bulk / mineral_bulk
    sat_bulk = dry_bulk + biot_ratio * biot_ratio / (porosity / fluid_bulk + (1.0 - porosity) / mineral_bulk - dry_bulk / (mineral_bulk * mineral_bulk))
    density = mineral_density * (1.0 - porosity) + porosity * (carbon_density * saturation + brine_density * (1.0 - saturation))
    return (sat_bulk + 4.0 / 3.0 * shear_mod) / density / velocity_ref - 1.0

def blend_matrix(positions, fraction, extent):
    columns = jnp.arange(extent, dtype=jnp.int32)[None, :]
    lower_w = (columns == positions[:, None]).astype(jnp.float32) * (1.0 - fraction)[:, None]
    upper_hit = (columns == (positions + 1)[:, None]) & (positions[:, None] >= 0)
    return lower_w + upper_hit.astype(jnp.float32) * fraction[:, None]

def laplace(values):
    padded = jnp.pad(values, 1)
    total = padded[2:, 1:-1, 1:-1] + padded[:-2, 1:-1, 1:-1]
    total = total + padded[1:-1, 2:, 1:-1] + padded[1:-1, :-2, 1:-1]
    total = total + padded[1:-1, 1:-1, 2:] + padded[1:-1, 1:-1, :-2]
    return total - 6.0 * values

def reference(right_side, storage, trans_x, trans_y, trans_z, well_cells, well_rates, sat_logit, porosity, y_index, y_frac, z_index, z_frac, background, wave_prev, wave_now, data_residual):
    source = jnp.zeros((NI * FY * FZ,), jnp.float32).at[well_cells].add(well_rates).reshape(NI, FY, FZ)
    forcing = right_side + source
    pressure = jnp.zeros_like(forcing)
    residual = forcing
    direction = forcing
    norm_now = jnp.sum(residual * residual)
    for number in range(ITERS):
        image = flow_apply(direction, storage, trans_x, trans_y, trans_z)
        alpha = norm_now / jnp.sum(direction * image)
        pressure = pressure + alpha * direction
        residual = residual - alpha * image
        norm_next = jnp.sum(residual * residual)
        direction = residual + norm_next / norm_now * direction
        norm_now = norm_next
    inflow = storage * pressure - flow_apply(pressure, storage, trans_x, trans_y, trans_z) + source
    saturation = jax.nn.sigmoid(sat_logit + transport * inflow)
    weight_y = blend_matrix(y_index, y_frac, NI)
    weight_z = blend_matrix(z_index, z_frac, FZ)

    def forward(sat_value):
        change = perturb(sat_value, porosity)
        depth = jnp.dot(change.reshape(NI * FY, FZ), weight_z.T, precision=lax.Precision.HIGHEST)
        lifted = jnp.dot(weight_y, depth.reshape(NI, FY * SZ), precision=lax.Precision.HIGHEST)
        model = background + lifted.reshape(SY, FY, SZ)
        previous, current = (wave_prev, wave_now)
        for number in range(STEPS):
            following = 2.0 * current - previous + courant * model * laplace(current)
            previous, current = (current, following)
        return current
    wavefield, pull = jax.vjp(forward, saturation)
    sat_gradient, = pull(data_residual)
    return (pressure, wavefield, sat_gradient)
```

```python
import functools

import jax
import jax.numpy as jnp
from jax import lax
from jax.experimental import pallas as pl
from jax.experimental.pallas import tpu as pltpu
from jax.sharding import PartitionSpec as P

courant = 0.25
transport = 2.0
velocity_ref = 22.5
mineral_bulk = 37.0
mineral_shear = 44.0
carbon_bulk = 0.08
brine_bulk = 2.5
mineral_density = 2.65
carbon_density = 0.7
brine_density = 1.03

F32 = jnp.float32
BF16 = jnp.bfloat16
NN = (((1,), (0,)), ((), ()))
NT = (((1,), (1,)), ((), ()))
CHUNKS = 4
ROWS = 64
PAD = 8


def split(value):
    high = value.astype(BF16)
    return high, (value - high.astype(F32)).astype(BF16)


def dot3(a_high, a_low, b_high, b_low, dims):
    def one(a, b):
        return lax.dot_general(a, b, dims, preferred_element_type=F32)

    return one(a_high, b_high) + (one(a_high, b_low) + one(a_low, b_high))


def perturb_and_slope(sat, por):
    solid = 1.0 - por
    frame = solid * solid * solid
    dry = mineral_bulk * frame
    shear = mineral_shear * frame
    biot = 1.0 - frame
    biot2 = biot * biot
    soft = sat * (1.0 / carbon_bulk) + (1.0 - sat) * (1.0 / brine_bulk)
    inv = 1.0 / (por * soft + solid * (1.0 / mineral_bulk) - dry * (1.0 / (mineral_bulk * mineral_bulk)))
    ratio = biot2 * inv
    total = dry + ratio + (4.0 / 3.0) * shear
    density = mineral_density * solid + por * (carbon_density * sat + brine_density * (1.0 - sat))
    inv_density = 1.0 / density
    change = total * inv_density * (1.0 / velocity_ref) - 1.0
    bulk_slope = -ratio * inv * por * (1.0 / carbon_bulk - 1.0 / brine_bulk)
    density_slope = por * (carbon_density - brine_density)
    slope = (bulk_slope - total * inv_density * density_slope) * inv_density * (1.0 / velocity_ref)
    return change, slope


def kernel(
    n, ni, fy, fz, sy, nx, sz,
    rs_h, st_h, tx_h, ty_h, tz_h, sl_h, po_h, bg_h, wp_h, wn_h, dr_h,
    cells, rates, yi_v, yf_v, zi_v, zf_v, yi_s, yf_s,
    pr_o, wf_o, sg_o,
    f, af, a2, src, st, tx, ty, tz, sl, po, chg, slope, pres, recv, depth, rest, ret,
    ua, ub, w5, w4, a5, a4, a3, l1, l2, mod, gz, wsend, wrecv, red,
    wzh, wzl, wyh, wyl,
    loc, hs, hr, ws, wr, rs_s, rs_r, as_s, as_r, out_s,
):
    me = lax.axis_index("sx")
    yc = sy // CHUNKS

    def wave_rows(ref):
        return ref.at[pl.ds(nx, sy * nx), :]

    def inner(ref):
        return ref.at[:, pl.ds(PAD, fy), :]

    loads = [
        pltpu.make_async_copy(a, b, loc.at[k])
        for k, (a, b) in enumerate(
            [
                (rs_h, f.at[pl.ds(1, ni), pl.ds(PAD, fy), :]),
                (st_h, st),
                (tx_h, tx),
                (ty_h, inner(ty)),
                (tz_h, tz),
                (wn_h, wave_rows(ub)),
                (sl_h, sl),
                (po_h, po),
                (bg_h, mod),
                (wp_h, wave_rows(ua)),
                (dr_h, a5),
            ]
        )
    ]
    for copy in loads:
        copy.start()

    barrier = pltpu.get_barrier_semaphore()

    def greet(o, _):
        pl.semaphore_signal(
            barrier, inc=1, device_id={"sx": lax.rem(me + o, n)},
            device_id_type=pl.DeviceIdType.MESH,
        )
        return 0

    lax.fori_loop(1, n, greet, 0)

    def remote(s, d, ssem, rsem, target):
        return pltpu.make_async_remote_copy(
            src_ref=s, dst_ref=d, send_sem=ssem, recv_sem=rsem,
            device_id={"sx": target}, device_id_type=pl.DeviceIdType.MESH,
        )

    has_left = me > 0
    has_right = me < n - 1

    def plane_copy(e, way):
        ref = (f, af)[e]
        here, there = ((1, ni + 1), (ni, 0))[way]
        return remote(
            ref.at[here, pl.ds(PAD, fy), :], ref.at[there, pl.ds(PAD, fy), :],
            hs.at[e, way], hr.at[e, way], me + (-1, 1)[way],
        )

    def wave_copy(e, q, way):
        if e == 0:
            s, d = wsend.at[e, way, q, 0], wrecv.at[e, 1 - way, q, 0]
        else:
            s, d = wsend.at[e, way, q], wrecv.at[e, 1 - way, q]
        return remote(s, d, ws.at[e, q, way], wr.at[e, q, way], me + (-1, 1)[way])

    def start_pair(make):
        pl.when(has_left)(lambda: make(0).start())
        pl.when(has_right)(lambda: make(1).start())

    def recv_pair(make):
        pl.when(has_right)(lambda: make(0).wait_recv())
        pl.when(has_left)(lambda: make(1).wait_recv())

    def sent_pair(make):
        pl.when(has_left)(lambda: make(0).wait_send())
        pl.when(has_right)(lambda: make(1).wait_send())

    rim = jnp.zeros((ni + 2, PAD, fz), F32)
    for ref in (f, af):
        ref[:, 0:PAD, :] = rim
        ref[:, PAD + fy:, :] = rim
    ty[:, 0:PAD, :] = rim[:ni]
    ty[:, PAD + fy:, :] = rim[:ni]
    zero_rows = jnp.zeros((nx, sz), F32)
    for ref in (ua, ub, w5, w4):
        ref[0:nx, :] = zero_rows
        ref[(sy + 1) * nx:, :] = zero_rows

    def zero_edge(plane, side):
        blank = jnp.zeros((fy, fz), F32)
        f[plane, pl.ds(PAD, fy), :] = blank
        af[plane, pl.ds(PAD, fy), :] = blank
        wrecv[:, side] = jnp.zeros((4, CHUNKS, 2, yc, sz), F32)

    pl.when(me == 0)(lambda: zero_edge(0, 0))
    pl.when(me == n - 1)(lambda: zero_edge(ni + 1, 1))

    cell_row = lax.shift_right_logical(cells[...], fz.bit_length() - 1)
    cell_col = cells[...] & (fz - 1)
    wells = cells.shape[1]
    rate_cols = jnp.where(
        lax.broadcasted_iota(jnp.int32, (fz, wells), 0) == cell_col, rates[...], 0.0
    )
    loads[0].wait()

    def well_plane(i):
        first = (me * ni + i) * fy
        hit = jnp.where(
            lax.broadcasted_iota(jnp.int32, (fy, wells), 0) + first == cell_row, 1.0, 0.0
        ).astype(F32)
        plane = lax.dot_general(
            hit, rate_cols, NT, precision=lax.Precision.HIGHEST, preferred_element_type=F32
        )
        src[i] = plane
        f[i + 1, pl.ds(PAD, fy), :] = f[i + 1, pl.ds(PAD, fy), :] + plane

    well_plane(0)
    well_plane(ni - 1)
    pl.semaphore_wait(barrier, n - 1)
    start_pair(functools.partial(plane_copy, 0))

    def mid_wells(i, _):
        well_plane(i)
        return 0

    lax.fori_loop(1, ni - 1, mid_wells, 0)

    row = lax.broadcasted_iota(jnp.int32, (fz, sz), 0)
    zi = zi_v[...]
    zf = zf_v[...]
    wz = jnp.where(row == zi, 1.0 - zf, 0.0) + jnp.where((row == zi + 1) & (zi >= 0), zf, 0.0)
    wzh[...], wzl[...] = split(wz)
    row = lax.broadcasted_iota(jnp.int32, (n * ni, sy), 0)
    yi = yi_v[...]
    yf = yf_v[...]
    wy = jnp.where(row == yi, 1.0 - yf, 0.0) + jnp.where((row == yi + 1) & (yi >= 0), yf, 0.0)
    wyh[...], wyl[...] = split(wy)

    for k in (1, 2, 3, 4):
        loads[k].wait()

    col = lax.broadcasted_iota(jnp.int32, (ROWS, fz), 1)

    def flow_apply(ref, i, j0):
        ext = ref[i, pl.ds(j0, ROWS + 2 * PAD), :]
        v = ext[PAD:PAD + ROWS]
        face = ty[i - 1, pl.ds(j0, ROWS + 2 * PAD), :] * (
            ext - pltpu.roll(ext, ROWS + 2 * PAD - 1, 0)
        )
        along_j = (face - pltpu.roll(face, 1, 0))[PAD:PAD + ROWS]
        up = jnp.where(col == fz - 1, 0.0, pltpu.roll(v, fz - 1, 1))
        face_z = tz[i - 1, pl.ds(j0, ROWS), :] * (v - up)
        along_k = face_z - jnp.where(col == 0, 0.0, pltpu.roll(face_z, 1, 1))
        mid = pl.ds(j0 + PAD, ROWS)
        along_i = tx[pl.ds(j0, ROWS), :] * (2.0 * v - ref[i + 1, mid, :] - ref[i - 1, mid, :])
        return v, st[i - 1, pl.ds(j0, ROWS), :] * v + along_i + along_j + along_k

    def fold(value):
        return jnp.sum(value.reshape(-1, 8, fz), axis=0)

    def image_plane(i, acc):
        def body(c, acc):
            j0 = pl.multiple_of(c * ROWS, ROWS)
            v, image = flow_apply(f, i, j0)
            af[i, pl.ds(j0 + PAD, ROWS), :] = image
            return acc[0] + fold(v * v), acc[1] + fold(v * image)

        return lax.fori_loop(0, fy // ROWS, body, acc)

    def image2_plane(i, _):
        def body(c, _):
            j0 = pl.multiple_of(c * ROWS, ROWS)
            a2[i - 1, pl.ds(j0, ROWS), :] = flow_apply(af, i, j0)[1]
            return 0

        return lax.fori_loop(0, fy // ROWS, body, 0)

    blank = jnp.zeros((8, fz), F32)
    acc = lax.fori_loop(2, ni, image_plane, (blank, blank))
    recv_pair(functools.partial(plane_copy, 0))
    acc = image_plane(1, acc)
    acc = image_plane(ni, acc)
    start_pair(functools.partial(plane_copy, 1))

    def red_copy(r, o):
        return remote(
            red.at[r, me], red.at[r, me], rs_s.at[r, o], rs_r.at[r, o], lax.rem(me + o, n)
        )

    def reduce_start(r, parts):
        rows = [jnp.sum(p, axis=0, keepdims=True) for p in parts]
        which = lax.broadcasted_iota(jnp.int32, (8, fz), 0)
        tile = jnp.zeros((8, fz), F32)
        for k, p in enumerate(rows):
            tile = jnp.where(which == k, p, tile)
        red[r, me] = tile

        def go(o, _):
            red_copy(r, o).start()
            return 0

        lax.fori_loop(1, n, go, 0)

    def reduce_end(r):
        def go(o, _):
            red_copy(r, o).wait_recv()
            return 0

        lax.fori_loop(1, n, go, 0)
        return jnp.sum(jnp.sum(red[r], axis=0), axis=1, keepdims=True)

    reduce_start(0, acc)
    lax.fori_loop(2, ni, image2_plane, 0)

    loads[5].wait()

    def first_edges(q, _):
        def body(t, _):
            for s in range(8):
                y = q * yc + t * 8 + s
                for way, x in ((0, 0), (1, nx - 1)):
                    line = ub[pl.ds(pl.multiple_of((y + 1) * nx, nx), nx), :][x:x + 1]
                    wsend[0, way, q, 0, pl.ds(t * 8 + s, 1), :] = line
            return 0

        lax.fori_loop(0, yc // 8, body, 0)
        start_pair(functools.partial(wave_copy, 0, q))
        return 0

    lax.fori_loop(0, CHUNKS, first_edges, 0)

    recv_pair(functools.partial(plane_copy, 1))
    image2_plane(1, 0)
    image2_plane(ni, 0)
    sums = reduce_end(0)
    norm0 = sums[0:1]
    curve0 = sums[1:2]
    alpha0 = norm0 / curve0

    def dots_plane(i, acc):
        def body(c, acc):
            j0 = pl.multiple_of(c * ROWS, ROWS)
            g = af[i + 1, pl.ds(j0 + PAD, ROWS), :]
            r1 = f[i + 1, pl.ds(j0 + PAD, ROWS), :] - alpha0 * g
            ar1 = g - alpha0 * a2[i, pl.ds(j0, ROWS), :]
            return acc[0] + fold(r1 * r1), acc[1] + fold(r1 * ar1), acc[2] + fold(r1 * g)

        return lax.fori_loop(0, fy // ROWS, body, acc)

    acc = lax.fori_loop(0, ni, dots_plane, (blank, blank, blank))
    reduce_start(1, acc)
    loads[6].wait()
    loads[7].wait()
    sums = reduce_end(1)
    norm1 = sums[0:1]
    beta = norm1 / norm0
    curve1 = sums[1:2] + 2.0 * beta * sums[2:3] + beta * beta * curve0
    alpha1 = norm1 / curve1
    c1 = alpha0 + alpha1 * (1.0 + beta)
    c2 = -alpha1 * alpha0

    def change_copy(o):
        d = lax.rem(me + o, n)
        return remote(
            chg.at[:, pl.ds(pl.multiple_of(d * nx, nx), nx), :],
            recv.at[pl.ds(pl.multiple_of(me * ni, ni), ni)],
            as_s.at[0, o], as_r.at[0, o], d,
        )

    def columns_of(d):
        j0 = pl.multiple_of(d * nx, nx)
        at = pl.ds(j0, nx)
        mid = pl.ds(pl.multiple_of(j0 + PAD, 8), nx)
        v = f[pl.ds(1, ni), mid, :]
        g = af[pl.ds(1, ni), mid, :]
        p = c1[0] * v + c2[0] * g
        ap = c1[0] * g + c2[0] * a2[:, at, :]
        inflow = st[:, at, :] * p - ap + src[:, at, :]
        sat = jax.nn.sigmoid(sl[:, at, :] + transport * inflow)
        value, gain = perturb_and_slope(sat, po[:, at, :])
        pres[:, at, :] = p
        slope[:, at, :] = gain
        return at, value

    def order(t):
        return 1 + lax.rem(t + n // 2 - 1, n - 1)

    def send_change(t, _):
        o = order(t)
        at, value = columns_of(lax.rem(me + o, n))
        chg[:, at, :] = value
        change_copy(o).start()
        return 0

    lax.fori_loop(0, n - 1, send_change, 0)
    _, value = columns_of(me)
    recv[pl.ds(pl.multiple_of(me * ni, ni), ni)] = value
    out_p = pltpu.make_async_copy(pres, pr_o, out_s.at[0])
    out_p.start()

    def blend_z(s):
        block = recv[pl.ds(pl.multiple_of(s * ni, ni), ni)].reshape(ni * nx, fz)
        high, low = split(block)
        depth[pl.ds(pl.multiple_of(s * ni, ni), ni)] = dot3(
            high, low, wzh[...], wzl[...], NN
        ).reshape(ni, nx, sz)

    blend_z(me)
    for k in (8, 9, 10):
        loads[k].wait()

    def take_change(t, _):
        o = order(t)
        change_copy(o).wait_recv()
        blend_z(lax.rem(me - o + n, n))
        return 0

    lax.fori_loop(0, n - 1, take_change, 0)

    zcol = lax.broadcasted_iota(jnp.int32, (nx, sz), 1)
    xrow = lax.broadcasted_iota(jnp.int32, (nx, sz), 0)

    def laplace(ref, y, low, high):
        here = pl.multiple_of((y + 1) * nx, nx)
        c = ref[pl.ds(here, nx), :]
        total = ref[pl.ds(pl.multiple_of(y * nx, nx), nx), :]
        total = total + ref[pl.ds(pl.multiple_of((y + 2) * nx, nx), nx), :]
        total = total + jnp.where(xrow == 0, low, pltpu.roll(c, 1, 0))
        total = total + jnp.where(xrow == nx - 1, high, pltpu.roll(c, nx - 1, 0))
        total = total + jnp.where(zcol == 0, 0.0, pltpu.roll(c, 1, 1))
        total = total + jnp.where(zcol == sz - 1, 0.0, pltpu.roll(c, sz - 1, 1))
        return c, total - 6.0 * c

    def stage(number):
        cur, old = ((ub, ua), (ua, ub))[(number - 1) % 2]
        e = number - 1
        w_in = (None, w5, w4, w5)[number - 1]
        w_out = (w5, w4, w5, None)[number - 1]

        def one(q, t, s, edges):
            line = t * 8 + s
            y = q * yc + line
            at = pl.ds(pl.multiple_of(y * nx, nx), nx)
            pad_at = pl.ds(pl.multiple_of((y + 1) * nx, nx), nx)
            if number == 1:
                index = yi_s[y]
                frac = yf_s[y]
                lower_w = jnp.where(index >= 0, 1.0 - frac, 0.0)
                upper_w = jnp.where(index >= 0, frac, 0.0)
                base = jnp.maximum(index, 0)
                lower = depth[base]
                upper = depth[base + 1]
                m = mod[at, :] + (lower_w * lower + upper_w * upper)
                mod[at, :] = m
            else:
                m = mod[at, :]
            c, lap = laplace(cur, y, edges[0][s:s + 1], edges[1][s:s + 1])
            new = 2.0 * c - old[pad_at, :] + courant * m * lap
            old[pad_at, :] = new
            if number == 1:
                l1[at, :] = lap
                adj = a5[at, :]
            else:
                _, lap_w = laplace(w_in, y, edges[2][s:s + 1], edges[3][s:s + 1])
                if number == 2:
                    adj = 2.0 * a5[at, :] + courant * lap_w
                    a4[at, :] = adj
                    l2[at, :] = lap
                elif number == 3:
                    late = a4[at, :]
                    adj = 2.0 * late + courant * lap_w - a5[at, :]
                    a3[at, :] = adj
                    l2[at, :] = l2[at, :] * adj + lap * late
                else:
                    adj = 2.0 * a3[at, :] + courant * lap_w - a4[at, :]
                    l1[at, :] = courant * (l1[at, :] * adj + l2[at, :] + lap * a5[at, :])
            if number < 4:
                w = m * adj
                w_out[pad_at, :] = w
                for way, x in ((0, 0), (1, nx - 1)):
                    wsend[e + 1, way, q, 0, pl.ds(line, 1), :] = new[x:x + 1]
                    wsend[e + 1, way, q, 1, pl.ds(line, 1), :] = w[x:x + 1]

        def chunk(q, _):
            recv_pair(functools.partial(wave_copy, e, q))

            def body(t, _):
                lines = pl.ds(pl.multiple_of(t * 8, 8), 8)
                edges = [
                    wrecv[e, side, q, what, lines, :]
                    for what in range(1 if number == 1 else 2)
                    for side in (0, 1)
                ]
                for s in range(8):
                    one(q, t, s, edges)
                return 0

            lax.fori_loop(0, yc // 8, body, 0)
            if number < 4:
                start_pair(functools.partial(wave_copy, e + 1, q))
            else:
                rows = pl.ds(pl.multiple_of(q * yc * nx, yc * nx), yc * nx)
                high, low = split(l1[rows, :])
                gz[rows, :] = dot3(high, low, wzh[...], wzl[...], NT)
            return 0

        lax.fori_loop(0, CHUNKS, chunk, 0)

    for number in (1, 2, 3, 4):
        stage(number)
    out_w = pltpu.make_async_copy(wave_rows(ub), wf_o, out_s.at[1])
    out_w.start()

    def restrict(x, _):
        high, low = split(gz[pl.ds(x, sy, stride=nx), :])
        rest[pl.ds(x, n * ni, stride=nx), :] = dot3(wyh[...], wyl[...], high, low, NN)
        return 0

    lax.fori_loop(0, nx, restrict, 0)

    def back_copy(o):
        d = lax.rem(me + o, n)
        return remote(
            rest.at[pl.ds(pl.multiple_of(d * ni * nx, ni * nx), ni * nx), :],
            ret.at[me], as_s.at[1, o], as_r.at[1, o], d,
        )

    def send_back(t, _):
        back_copy(order(t)).start()
        return 0

    lax.fori_loop(0, n - 1, send_back, 0)

    def finish(s, block):
        at = pl.ds(pl.multiple_of(s * nx, nx), nx)
        slope[:, at, :] = slope[:, at, :] * block.reshape(ni, nx, fz)

    finish(me, rest[pl.ds(pl.multiple_of(me * ni * nx, ni * nx), ni * nx), :])

    def take_back(t, _):
        o = order(t)
        back_copy(o).wait_recv()
        s = lax.rem(me - o + n, n)
        finish(s, ret[s])
        return 0

    lax.fori_loop(0, n - 1, take_back, 0)
    out_g = pltpu.make_async_copy(slope, sg_o, out_s.at[2])
    out_g.start()

    for e in range(2):
        sent_pair(functools.partial(plane_copy, e))

    def sent_waves(q, _):
        for e in range(4):
            sent_pair(functools.partial(wave_copy, e, q))
        return 0

    lax.fori_loop(0, CHUNKS, sent_waves, 0)

    def sent_all(o, _):
        red_copy(0, o).wait_send()
        red_copy(1, o).wait_send()
        change_copy(o).wait_send()
        back_copy(o).wait_send()
        return 0

    lax.fori_loop(1, n, sent_all, 0)
    out_p.wait()
    out_w.wait()
    out_g.wait()


def per_device(
    n, right_side, storage, trans_x, trans_y, trans_z, well_cells, well_rates, sat_logit, porosity,
    y_index, y_frac, z_index, z_frac, background, wave_prev, wave_now, data_residual,
):
    ni, fy, fz = right_side.shape
    sy, nx, sz = background.shape
    cells = ni * n
    flat = sy * nx

    def vm(*shape, dtype=F32):
        return pltpu.VMEM(shape, dtype)

    wide = (sy + 2) * nx
    scratch = [
        vm(ni + 2, fy + 2 * PAD, fz), vm(ni + 2, fy + 2 * PAD, fz), vm(ni, fy, fz), vm(ni, fy, fz),
        vm(ni, fy, fz), vm(fy, fz), vm(ni, fy + 2 * PAD, fz), vm(ni, fy, fz), vm(ni, fy, fz),
        vm(ni, fy, fz), vm(ni, fy, fz), vm(ni, fy, fz), vm(ni, fy, fz),
        vm(cells, nx, fz), vm(cells, nx, sz), vm(cells * nx, fz), vm(n, ni * nx, fz),
        vm(wide, sz), vm(wide, sz), vm(wide, sz), vm(wide, sz),
        vm(flat, sz), vm(flat, sz), vm(flat, sz), vm(flat, sz), vm(flat, sz), vm(flat, sz),
        vm(flat, fz),
        vm(4, 2, CHUNKS, 2, sy // CHUNKS, sz), vm(4, 2, CHUNKS, 2, sy // CHUNKS, sz),
        vm(2, n, 8, fz),
        vm(fz, sz, dtype=BF16), vm(fz, sz, dtype=BF16), vm(cells, sy, dtype=BF16), vm(cells, sy, dtype=BF16),
    ]
    dma = pltpu.SemaphoreType.DMA
    scratch += [
        dma((11,)), dma((2, 2)), dma((2, 2)), dma((4, CHUNKS, 2)), dma((4, CHUNKS, 2)),
        dma((2, n)), dma((2, n)), dma((2, n)), dma((2, n)), dma((3,)),
    ]
    any_spec = pl.BlockSpec(memory_space=pl.ANY)
    vmem_spec = pl.BlockSpec(memory_space=pltpu.VMEM)
    smem_spec = pl.BlockSpec(memory_space=pltpu.SMEM)
    pressure, wavefield, sat_gradient = pl.pallas_call(
        functools.partial(kernel, n, ni, fy, fz, sy, nx, sz),
        out_shape=(
            jax.ShapeDtypeStruct((ni, fy, fz), F32),
            jax.ShapeDtypeStruct((flat, sz), F32),
            jax.ShapeDtypeStruct((ni, fy, fz), F32),
        ),
        in_specs=[any_spec] * 11 + [vmem_spec] * 6 + [smem_spec] * 2,
        out_specs=(any_spec,) * 3,
        scratch_shapes=scratch,
        compiler_params=pltpu.CompilerParams(
            collective_id=0, has_side_effects=True, vmem_limit_bytes=60 * 1024 * 1024
        ),
        cost_estimate=pl.CostEstimate(flops=200000000, bytes_accessed=14000000, transcendentals=200000),
    )(
        right_side, storage, trans_x, trans_y, trans_z, sat_logit, porosity,
        background.reshape(flat, sz), wave_prev.reshape(flat, sz), wave_now.reshape(flat, sz),
        data_residual.reshape(flat, sz),
        well_cells.reshape(1, -1), well_rates.reshape(1, -1),
        y_index.reshape(1, -1), y_frac.reshape(1, -1), z_index.reshape(1, -1), z_frac.reshape(1, -1),
        y_index, y_frac,
    )
    return pressure, wavefield.reshape(sy, nx, sz), sat_gradient


def solution(mesh):
    cells = P(("grp", "sx"), None, None)
    waves = P(None, ("grp", "sx"), None)
    in_specs = (
        cells, cells, P("grp", None), cells, cells, P("grp"), P("grp"), cells, cells,
        P(), P(), P(), P(), waves, waves, waves, waves,
    )
    return jax.shard_map(
        functools.partial(per_device, mesh.shape["sx"]),
        mesh=mesh, in_specs=in_specs, out_specs=(cells, waves, cells), check_vma=False,
    )
```

```python
import functools

import jax
import jax.numpy as jnp
from jax import lax
from jax.experimental import pallas as pl
from jax.experimental.pallas import tpu as pltpu
from jax.sharding import PartitionSpec as P

courant = 0.25
transport = 2.0
velocity_ref = 22.5
mineral_bulk = 37.0
mineral_shear = 44.0
carbon_bulk = 0.08
brine_bulk = 2.5
mineral_density = 2.65
carbon_density = 0.7
brine_density = 1.03

F32 = jnp.float32
BF16 = jnp.bfloat16
NN = (((1,), (0,)), ((), ()))
NT = (((1,), (1,)), ((), ()))
CHUNKS = 4
ROWS = 64
PAD = 8
MOVES = 4


def split(value):
    high = value.astype(BF16)
    return high, (value - high.astype(F32)).astype(BF16)


def dot3(a_high, a_low, b_high, b_low, dims):
    def one(a, b):
        return lax.dot_general(a, b, dims, preferred_element_type=F32)

    return one(a_high, b_high) + (one(a_high, b_low) + one(a_low, b_high))


def perturb_and_slope(sat, por):
    solid = 1.0 - por
    frame = solid * solid * solid
    dry = mineral_bulk * frame
    shear = mineral_shear * frame
    biot = 1.0 - frame
    biot2 = biot * biot
    soft = sat * (1.0 / carbon_bulk) + (1.0 - sat) * (1.0 / brine_bulk)
    inv = 1.0 / (por * soft + solid * (1.0 / mineral_bulk) - dry * (1.0 / (mineral_bulk * mineral_bulk)))
    ratio = biot2 * inv
    total = dry + ratio + (4.0 / 3.0) * shear
    density = mineral_density * solid + por * (carbon_density * sat + brine_density * (1.0 - sat))
    inv_density = 1.0 / density
    change = total * inv_density * (1.0 / velocity_ref) - 1.0
    bulk_slope = -ratio * inv * por * (1.0 / carbon_bulk - 1.0 / brine_bulk)
    density_slope = por * (carbon_density - brine_density)
    slope = (bulk_slope - total * inv_density * density_slope) * inv_density * (1.0 / velocity_ref)
    return change, slope


def kernel(
    n, ni, fy, fz, sy, nx, sz,
    rs_h, st_h, tx_h, ty_h, tz_h, sl_h, po_h, bg_h, wp_h, wn_h, dr_h,
    cells, rates, yi_v, yf_v, zi_v, zf_v, yi_s, yf_s,
    pr_o, wf_o, sg_o,
    f, af, a2, src, st, tx, ty, tz, sl, po, chg, slope, pres, recv, depth, rest, ret,
    ua, ub, w5, w4, a5, a4, a3, l1, l2, mod, grad, gz, wsend, wrecv, red,
    wzh, wzl, wyh, wyl,
    loc, hs, hr, ws, wr, rs_s, rs_r, as_s, as_r, out_s,
):
    me = lax.axis_index("sx")
    yc = sy // CHUNKS
    hx = nx // 2

    def wave_rows(ref):
        return ref.at[pl.ds(nx, sy * nx), :]

    def inner(ref):
        return ref.at[:, pl.ds(PAD, fy), :]

    loads = [
        pltpu.make_async_copy(a, b, loc.at[k])
        for k, (a, b) in enumerate(
            [
                (rs_h, f.at[pl.ds(1, ni), pl.ds(PAD, fy), :]),
                (st_h, st),
                (tx_h, tx),
                (ty_h, inner(ty)),
                (tz_h, tz),
                (wn_h, wave_rows(ub)),
                (sl_h, sl),
                (po_h, po),
                (bg_h, mod),
                (wp_h, wave_rows(ua)),
                (dr_h, a5),
            ]
        )
    ]
    for copy in loads:
        copy.start()

    barrier = pltpu.get_barrier_semaphore()

    def greet(o, _):
        pl.semaphore_signal(
            barrier, inc=1, device_id={"sx": lax.rem(me + o, n)},
            device_id_type=pl.DeviceIdType.MESH,
        )
        return 0

    lax.fori_loop(1, n, greet, 0)

    def remote(s, d, ssem, rsem, target):
        return pltpu.make_async_remote_copy(
            src_ref=s, dst_ref=d, send_sem=ssem, recv_sem=rsem,
            device_id={"sx": target}, device_id_type=pl.DeviceIdType.MESH,
        )

    has_left = me > 0
    has_right = me < n - 1

    def plane_copy(e, way):
        ref = (f, af)[e]
        here, there = ((1, ni + 1), (ni, 0))[way]
        return remote(
            ref.at[here, pl.ds(PAD, fy), :], ref.at[there, pl.ds(PAD, fy), :],
            hs.at[e, way], hr.at[e, way], me + (-1, 1)[way],
        )

    def wave_copy(e, q, way):
        if e == 0:
            s, d = wsend.at[e, way, q, 0], wrecv.at[e, 1 - way, q, 0]
        else:
            s, d = wsend.at[e, way, q], wrecv.at[e, 1 - way, q]
        return remote(s, d, ws.at[e, q, way], wr.at[e, q, way], me + (-1, 1)[way])

    def start_pair(make):
        pl.when(has_left)(lambda: make(0).start())
        pl.when(has_right)(lambda: make(1).start())

    def recv_pair(make):
        pl.when(has_right)(lambda: make(0).wait_recv())
        pl.when(has_left)(lambda: make(1).wait_recv())

    def start_way(make, way):
        pl.when((has_left, has_right)[way])(lambda: make(way).start())

    def recv_side(make, side):
        pl.when((has_left, has_right)[side])(lambda: make(1 - side).wait_recv())

    def sent_pair(make):
        pl.when(has_left)(lambda: make(0).wait_send())
        pl.when(has_right)(lambda: make(1).wait_send())

    rim = jnp.zeros((ni + 2, PAD, fz), F32)
    for ref in (f, af):
        ref[:, 0:PAD, :] = rim
        ref[:, PAD + fy:, :] = rim
    ty[:, 0:PAD, :] = rim[:ni]
    ty[:, PAD + fy:, :] = rim[:ni]
    zero_rows = jnp.zeros((nx, sz), F32)
    for ref in (ua, ub, w5, w4):
        ref[0:nx, :] = zero_rows
        ref[(sy + 1) * nx:, :] = zero_rows

    def zero_edge(plane, side):
        blank = jnp.zeros((fy, fz), F32)
        f[plane, pl.ds(PAD, fy), :] = blank
        af[plane, pl.ds(PAD, fy), :] = blank
        wrecv[:, side] = jnp.zeros((4, CHUNKS, 2, yc, sz), F32)

    pl.when(me == 0)(lambda: zero_edge(0, 0))
    pl.when(me == n - 1)(lambda: zero_edge(ni + 1, 1))

    cell_row = lax.shift_right_logical(cells[...], fz.bit_length() - 1)
    cell_col = cells[...] & (fz - 1)
    wells = cells.shape[1]
    rate_cols = jnp.where(
        lax.broadcasted_iota(jnp.int32, (fz, wells), 0) == cell_col, rates[...], 0.0
    )
    loads[0].wait()

    def well_plane(i):
        first = (me * ni + i) * fy
        hit = jnp.where(
            lax.broadcasted_iota(jnp.int32, (fy, wells), 0) + first == cell_row, 1.0, 0.0
        ).astype(F32)
        plane = lax.dot_general(
            hit, rate_cols, NT, precision=lax.Precision.HIGHEST, preferred_element_type=F32
        )
        src[i] = plane
        f[i + 1, pl.ds(PAD, fy), :] = f[i + 1, pl.ds(PAD, fy), :] + plane

    well_plane(0)
    well_plane(ni - 1)
    pl.semaphore_wait(barrier, n - 1)
    start_pair(functools.partial(plane_copy, 0))

    def mid_wells(i, _):
        well_plane(i)
        return 0

    lax.fori_loop(1, ni - 1, mid_wells, 0)

    row = lax.broadcasted_iota(jnp.int32, (fz, sz), 0)
    zi = zi_v[...]
    zf = zf_v[...]
    wz = jnp.where(row == zi, 1.0 - zf, 0.0) + jnp.where((row == zi + 1) & (zi >= 0), zf, 0.0)
    wzh[...], wzl[...] = split(wz)
    row = lax.broadcasted_iota(jnp.int32, (n * ni, sy), 0)
    yi = yi_v[...]
    yf = yf_v[...]
    wy = jnp.where(row == yi, 1.0 - yf, 0.0) + jnp.where((row == yi + 1) & (yi >= 0), yf, 0.0)
    wyh[...], wyl[...] = split(wy)

    for k in (1, 2, 3, 4):
        loads[k].wait()

    col = lax.broadcasted_iota(jnp.int32, (ROWS, fz), 1)

    def flow_apply(ref, i, j0):
        ext = ref[i, pl.ds(j0, ROWS + 2 * PAD), :]
        v = ext[PAD:PAD + ROWS]
        face = ty[i - 1, pl.ds(j0, ROWS + 2 * PAD), :] * (
            ext - pltpu.roll(ext, ROWS + 2 * PAD - 1, 0)
        )
        along_j = (face - pltpu.roll(face, 1, 0))[PAD:PAD + ROWS]
        up = jnp.where(col == fz - 1, 0.0, pltpu.roll(v, fz - 1, 1))
        face_z = tz[i - 1, pl.ds(j0, ROWS), :] * (v - up)
        along_k = face_z - jnp.where(col == 0, 0.0, pltpu.roll(face_z, 1, 1))
        mid = pl.ds(j0 + PAD, ROWS)
        along_i = tx[pl.ds(j0, ROWS), :] * (2.0 * v - ref[i + 1, mid, :] - ref[i - 1, mid, :])
        return v, st[i - 1, pl.ds(j0, ROWS), :] * v + along_i + along_j + along_k

    def fold(value):
        return jnp.sum(value.reshape(-1, 8, fz), axis=0)

    def image_plane(i, acc):
        def body(c, acc):
            j0 = pl.multiple_of(c * ROWS, ROWS)
            v, image = flow_apply(f, i, j0)
            af[i, pl.ds(j0 + PAD, ROWS), :] = image
            return acc[0] + fold(v * v), acc[1] + fold(v * image)

        return lax.fori_loop(0, fy // ROWS, body, acc)

    def image2_plane(i, _):
        def body(c, _):
            j0 = pl.multiple_of(c * ROWS, ROWS)
            a2[i - 1, pl.ds(j0, ROWS), :] = flow_apply(af, i, j0)[1]
            return 0

        return lax.fori_loop(0, fy // ROWS, body, 0)

    blank = jnp.zeros((8, fz), F32)
    acc = lax.fori_loop(2, ni, image_plane, (blank, blank))
    recv_pair(functools.partial(plane_copy, 0))
    acc = image_plane(1, acc)
    acc = image_plane(ni, acc)
    start_pair(functools.partial(plane_copy, 1))

    def red_copy(r, o):
        return remote(
            red.at[r, me], red.at[r, me], rs_s.at[r, o], rs_r.at[r, o], lax.rem(me + o, n)
        )

    def reduce_start(r, parts):
        rows = [jnp.sum(p, axis=0, keepdims=True) for p in parts]
        which = lax.broadcasted_iota(jnp.int32, (8, fz), 0)
        tile = jnp.zeros((8, fz), F32)
        for k, p in enumerate(rows):
            tile = jnp.where(which == k, p, tile)
        red[r, me] = tile

        def go(o, _):
            red_copy(r, o).start()
            return 0

        lax.fori_loop(1, n, go, 0)

    def reduce_end(r):
        def go(o, _):
            red_copy(r, o).wait_recv()
            return 0

        lax.fori_loop(1, n, go, 0)
        return jnp.sum(jnp.sum(red[r], axis=0), axis=1, keepdims=True)

    reduce_start(0, acc)
    lax.fori_loop(2, ni, image2_plane, 0)

    loads[5].wait()

    def first_edges(q, _):
        def body(t, _):
            for s in range(8):
                y = q * yc + t * 8 + s
                for way, x in ((0, 0), (1, nx - 1)):
                    line = ub[pl.ds(pl.multiple_of((y + 1) * nx, nx), nx), :][x:x + 1]
                    wsend[0, way, q, 0, pl.ds(t * 8 + s, 1), :] = line
            return 0

        lax.fori_loop(0, yc // 8, body, 0)
        start_pair(functools.partial(wave_copy, 0, q))
        return 0

    lax.fori_loop(0, CHUNKS, first_edges, 0)

    recv_pair(functools.partial(plane_copy, 1))
    image2_plane(1, 0)
    image2_plane(ni, 0)
    sums = reduce_end(0)
    norm0 = sums[0:1]
    curve0 = sums[1:2]
    alpha0 = norm0 / curve0

    def dots_plane(i, acc):
        def body(c, acc):
            j0 = pl.multiple_of(c * ROWS, ROWS)
            g = af[i + 1, pl.ds(j0 + PAD, ROWS), :]
            r1 = f[i + 1, pl.ds(j0 + PAD, ROWS), :] - alpha0 * g
            ar1 = g - alpha0 * a2[i, pl.ds(j0, ROWS), :]
            return acc[0] + fold(r1 * r1), acc[1] + fold(r1 * ar1), acc[2] + fold(r1 * g)

        return lax.fori_loop(0, fy // ROWS, body, acc)

    acc = lax.fori_loop(0, ni, dots_plane, (blank, blank, blank))
    reduce_start(1, acc)

    zcol = lax.broadcasted_iota(jnp.int32, (nx, sz), 1)
    xrow = lax.broadcasted_iota(jnp.int32, (nx, sz), 0)

    def laplace(ref, y, low, high):
        here = pl.multiple_of((y + 1) * nx, nx)
        c = ref[pl.ds(here, nx), :]
        total = ref[pl.ds(pl.multiple_of(y * nx, nx), nx), :]
        total = total + ref[pl.ds(pl.multiple_of((y + 2) * nx, nx), nx), :]
        total = total + jnp.where(xrow == 0, low, pltpu.roll(c, 1, 0))
        total = total + jnp.where(xrow == nx - 1, high, pltpu.roll(c, nx - 1, 0))
        total = total + jnp.where(zcol == 0, 0.0, pltpu.roll(c, 1, 1))
        total = total + jnp.where(zcol == sz - 1, 0.0, pltpu.roll(c, sz - 1, 1))
        return c, total - 6.0 * c

    def first_stencil(q, _):
        recv_pair(functools.partial(wave_copy, 0, q))

        def body(t, _):
            lines = pl.ds(pl.multiple_of(t * 8, 8), 8)
            low = wrecv[0, 0, q, 0, lines, :]
            high = wrecv[0, 1, q, 0, lines, :]
            for s in range(8):
                y = q * yc + t * 8 + s
                _, lap = laplace(ub, y, low[s:s + 1], high[s:s + 1])
                l1[pl.ds(pl.multiple_of(y * nx, nx), nx), :] = lap
            return 0

        lax.fori_loop(0, yc // 8, body, 0)
        return 0

    lax.fori_loop(0, CHUNKS, first_stencil, 0)
    for k in (6, 7, 8, 9, 10):
        loads[k].wait()
    sums = reduce_end(1)
    norm1 = sums[0:1]
    beta = norm1 / norm0
    curve1 = sums[1:2] + 2.0 * beta * sums[2:3] + beta * beta * curve0
    alpha1 = norm1 / curve1
    c1 = alpha0 + alpha1 * (1.0 + beta)
    c2 = -alpha1 * alpha0

    def change_copy(o, h):
        d = lax.rem(me + o, n)
        return remote(
            chg.at[:, pl.ds(pl.multiple_of(d * nx + h * hx, hx), hx), :],
            recv.at[h, pl.ds(pl.multiple_of(me * ni, ni), ni)],
            as_s.at[h, o], as_r.at[h, o], d,
        )

    def columns_of(d, h):
        j0 = pl.multiple_of(d * nx + h * hx, hx)
        at = pl.ds(j0, hx)
        mid = pl.ds(pl.multiple_of(j0 + PAD, 8), hx)
        v = f[pl.ds(1, ni), mid, :]
        g = af[pl.ds(1, ni), mid, :]
        p = c1[0] * v + c2[0] * g
        ap = c1[0] * g + c2[0] * a2[:, at, :]
        inflow = st[:, at, :] * p - ap + src[:, at, :]
        sat = jax.nn.sigmoid(sl[:, at, :] + transport * inflow)
        value, gain = perturb_and_slope(sat, po[:, at, :])
        pres[:, at, :] = p
        slope[:, at, :] = gain
        return at, value

    def order(t):
        return 1 + lax.rem(t + n // 2 - 1, n - 1)

    for h in (0, 1):

        def send_change(t, _):
            o = order(t)
            at, value = columns_of(lax.rem(me + o, n), h)
            chg[:, at, :] = value
            change_copy(o, h).start()
            return 0

        lax.fori_loop(0, n - 1, send_change, 0)
    for h in (0, 1):
        _, value = columns_of(me, h)
        recv[h, pl.ds(pl.multiple_of(me * ni, ni), ni)] = value
    out_p = pltpu.make_async_copy(pres, pr_o, out_s.at[0])
    out_p.start()

    group = n * ni // 2

    def first_step(h):
        def take_change(t, _):
            change_copy(order(t), h).wait_recv()
            return 0

        lax.fori_loop(0, n - 1, take_change, 0)

        def blend_z(b, _):
            at = pl.ds(pl.multiple_of(b * group, group), group)
            high, low = split(recv[h, at].reshape(group * hx, fz))
            depth[h, at] = dot3(high, low, wzh[...], wzl[...], NN).reshape(group, hx, sz)
            return 0

        lax.fori_loop(0, 2, blend_z, 0)
        x = (0, hx - 1)[h]

        def chunk(q, _):
            def body(t, _):
                for s in range(8):
                    line = t * 8 + s
                    y = q * yc + line
                    at = pl.ds(pl.multiple_of(y * nx + h * hx, hx), hx)
                    pad_at = pl.ds(pl.multiple_of((y + 1) * nx + h * hx, hx), hx)
                    index = yi_s[y]
                    frac = yf_s[y]
                    lower_w = jnp.where(index >= 0, 1.0 - frac, 0.0)
                    upper_w = jnp.where(index >= 0, frac, 0.0)
                    base = jnp.maximum(index, 0)
                    lower = depth[h, base]
                    upper = depth[h, base + 1]
                    m = mod[at, :] + (lower_w * lower + upper_w * upper)
                    mod[at, :] = m
                    new = 2.0 * ub[pad_at, :] - ua[pad_at, :] + courant * m * l1[at, :]
                    w = m * a5[at, :]
                    ua[pad_at, :] = new
                    w5[pad_at, :] = w
                    wsend[1, h, q, 0, pl.ds(line, 1), :] = new[x:x + 1]
                    wsend[1, h, q, 1, pl.ds(line, 1), :] = w[x:x + 1]
                return 0

            lax.fori_loop(0, yc // 8, body, 0)
            start_way(functools.partial(wave_copy, 1, q), h)
            return 0

        lax.fori_loop(0, CHUNKS, chunk, 0)

    first_step(0)
    first_step(1)

    def middle_step(number):
        cur, old = ((ub, ua), (ua, ub))[(number - 1) % 2]
        w_in, w_out = ((w5, w4), (w4, w5))[number - 2]
        e = number - 1

        def chunk(q, _):
            recv_pair(functools.partial(wave_copy, e, q))

            def body(t, _):
                lines = pl.ds(pl.multiple_of(t * 8, 8), 8)
                edges = [
                    wrecv[e, side, q, what, lines, :] for what in range(2) for side in (0, 1)
                ]
                for s in range(8):
                    line = t * 8 + s
                    y = q * yc + line
                    at = pl.ds(pl.multiple_of(y * nx, nx), nx)
                    pad_at = pl.ds(pl.multiple_of((y + 1) * nx, nx), nx)
                    m = mod[at, :]
                    c, lap = laplace(cur, y, edges[0][s:s + 1], edges[1][s:s + 1])
                    new = 2.0 * c - old[pad_at, :] + courant * m * lap
                    _, lap_w = laplace(w_in, y, edges[2][s:s + 1], edges[3][s:s + 1])
                    if number == 2:
                        adj = 2.0 * a5[at, :] + courant * lap_w
                        a4[at, :] = adj
                        l2[at, :] = lap
                    else:
                        late = a4[at, :]
                        adj = 2.0 * late + courant * lap_w - a5[at, :]
                        a3[at, :] = adj
                        l2[at, :] = l2[at, :] * adj + lap * late
                    w = m * adj
                    old[pad_at, :] = new
                    w_out[pad_at, :] = w
                    for way, x in ((0, 0), (1, nx - 1)):
                        wsend[e + 1, way, q, 0, pl.ds(line, 1), :] = new[x:x + 1]
                        wsend[e + 1, way, q, 1, pl.ds(line, 1), :] = w[x:x + 1]
                return 0

            lax.fori_loop(0, yc // 8, body, 0)
            start_pair(functools.partial(wave_copy, e + 1, q))
            return 0

        lax.fori_loop(0, CHUNKS, chunk, 0)

    middle_step(2)
    middle_step(3)

    hcol = lax.broadcasted_iota(jnp.int32, (hx, sz), 1)
    hrow = lax.broadcasted_iota(jnp.int32, (hx, sz), 0)

    def half_laplace(ref, y, h, edge):
        def part(row, g):
            return ref[pl.ds(pl.multiple_of(row * nx + g * hx, hx), hx), :]

        c = part(y + 1, h)
        other = part(y + 1, 1 - h)
        low, high = ((edge, other[0:1]), (other[hx - 1:hx], edge))[h]
        total = part(y, h) + part(y + 2, h)
        total = total + jnp.where(hrow == 0, low, pltpu.roll(c, 1, 0))
        total = total + jnp.where(hrow == hx - 1, high, pltpu.roll(c, hx - 1, 0))
        total = total + jnp.where(hcol == 0, 0.0, pltpu.roll(c, 1, 1))
        total = total + jnp.where(hcol == sz - 1, 0.0, pltpu.roll(c, sz - 1, 1))
        return total - 6.0 * c

    def back_copy(o, h):
        d = lax.rem(me + o, n)
        size = ni * hx
        return remote(
            rest.at[h, pl.ds(pl.multiple_of(d * size, size), size), :],
            ret.at[h, me], as_s.at[2 + h, o], as_r.at[2 + h, o], d,
        )

    def last_step(h):
        def chunk(q, _):
            recv_side(functools.partial(wave_copy, 3, q), h)

            def body(t, _):
                lines = pl.ds(pl.multiple_of(t * 8, 8), 8)
                edge_u = wrecv[3, h, q, 0, lines, :]
                edge_w = wrecv[3, h, q, 1, lines, :]
                for s in range(8):
                    y = q * yc + t * 8 + s
                    at = pl.ds(pl.multiple_of(y * nx + h * hx, hx), hx)
                    lap = half_laplace(ua, y, h, edge_u[s:s + 1])
                    lap_w = half_laplace(w5, y, h, edge_w[s:s + 1])
                    adj = 2.0 * a3[at, :] + courant * lap_w - a4[at, :]
                    grad[h, pl.ds(pl.multiple_of(y * hx, hx), hx), :] = courant * (
                        l1[at, :] * adj + l2[at, :] + lap * a5[at, :]
                    )
                    l2[at, :] = lap
                return 0

            lax.fori_loop(0, yc // 8, body, 0)
            rows = pl.ds(pl.multiple_of(q * yc * hx, yc * hx), yc * hx)
            high, low = split(grad[h, rows, :])
            gz[h, rows, :] = dot3(high, low, wzh[...], wzl[...], NT)
            return 0

        lax.fori_loop(0, CHUNKS, chunk, 0)

        for x in range(hx):
            high, low = split(gz[h, pl.ds(x, sy, stride=hx), :])
            rest[h, pl.ds(x, n * ni, stride=hx), :] = dot3(wyh[...], wyl[...], high, low, NN)

        def send_back(t, _):
            back_copy(order(t), h).start()
            return 0

        lax.fori_loop(0, n - 1, send_back, 0)

    last_step(0)
    last_step(1)

    def last_wave(t, _):
        rows = 8 * nx
        at = pl.ds(pl.multiple_of(t * rows, rows), rows)
        pad_at = pl.ds(pl.multiple_of(t * rows + nx, nx), rows)
        ub[pad_at, :] = 2.0 * ua[pad_at, :] - ub[pad_at, :] + courant * mod[at, :] * l2[at, :]
        return 0

    lax.fori_loop(0, sy // 8, last_wave, 0)
    out_w = pltpu.make_async_copy(wave_rows(ub), wf_o, out_s.at[1])
    out_w.start()

    def finish(s, h, block):
        at = pl.ds(pl.multiple_of(s * nx + h * hx, hx), hx)
        slope[:, at, :] = slope[:, at, :] * block.reshape(ni, hx, fz)

    for h in (0, 1):
        size = ni * hx
        finish(me, h, rest[h, pl.ds(pl.multiple_of(me * size, size), size), :])

        def take_back(t, _):
            o = order(t)
            back_copy(o, h).wait_recv()
            s = lax.rem(me - o + n, n)
            finish(s, h, ret[h, s])
            return 0

        lax.fori_loop(0, n - 1, take_back, 0)
    out_g = pltpu.make_async_copy(slope, sg_o, out_s.at[2])
    out_g.start()

    for e in range(2):
        sent_pair(functools.partial(plane_copy, e))

    def sent_waves(q, _):
        for e in range(4):
            sent_pair(functools.partial(wave_copy, e, q))
        return 0

    lax.fori_loop(0, CHUNKS, sent_waves, 0)

    def sent_all(o, _):
        red_copy(0, o).wait_send()
        red_copy(1, o).wait_send()
        for h in (0, 1):
            change_copy(o, h).wait_send()
            back_copy(o, h).wait_send()
        return 0

    lax.fori_loop(1, n, sent_all, 0)
    out_p.wait()
    out_w.wait()
    out_g.wait()


def move_out(*refs):
    ins, outs, held, arrive, leave = refs[:3], refs[3:6], refs[6:9], refs[9], refs[10]
    moves = []
    for k in range(3):
        for part in range(MOVES):
            rows = ins[k].shape[0] // MOVES
            at = pl.ds(part * rows, rows)
            moves.append(
                (
                    pltpu.make_async_copy(ins[k].at[at], held[k].at[at], arrive.at[k, part]),
                    pltpu.make_async_copy(held[k].at[at], outs[k].at[at], leave.at[k, part]),
                )
            )
    for come, _ in moves:
        come.start()
    for come, go in moves:
        come.wait()
        go.start()
    for _, go in moves:
        go.wait()


def per_device(
    n, right_side, storage, trans_x, trans_y, trans_z, well_cells, well_rates, sat_logit, porosity,
    y_index, y_frac, z_index, z_frac, background, wave_prev, wave_now, data_residual,
):
    ni, fy, fz = right_side.shape
    sy, nx, sz = background.shape
    cells = ni * n
    flat = sy * nx

    def vm(*shape, dtype=F32):
        return pltpu.VMEM(shape, dtype)

    wide = (sy + 2) * nx
    scratch = [
        vm(ni + 2, fy + 2 * PAD, fz), vm(ni + 2, fy + 2 * PAD, fz), vm(ni, fy, fz), vm(ni, fy, fz),
        vm(ni, fy, fz), vm(fy, fz), vm(ni, fy + 2 * PAD, fz), vm(ni, fy, fz), vm(ni, fy, fz),
        vm(ni, fy, fz), vm(ni, fy, fz), vm(ni, fy, fz), vm(ni, fy, fz),
        vm(2, cells, nx // 2, fz), vm(2, cells, nx // 2, sz), vm(2, cells * nx // 2, fz),
        vm(2, n, ni * nx // 2, fz),
        vm(wide, sz), vm(wide, sz), vm(wide, sz), vm(wide, sz),
        vm(flat, sz), vm(flat, sz), vm(flat, sz), vm(flat, sz), vm(flat, sz), vm(flat, sz),
        vm(2, flat // 2, sz), vm(2, flat // 2, fz),
        vm(4, 2, CHUNKS, 2, sy // CHUNKS, sz), vm(4, 2, CHUNKS, 2, sy // CHUNKS, sz),
        vm(2, n, 8, fz),
        vm(fz, sz, dtype=BF16), vm(fz, sz, dtype=BF16), vm(cells, sy, dtype=BF16), vm(cells, sy, dtype=BF16),
    ]
    dma = pltpu.SemaphoreType.DMA
    scratch += [
        dma((11,)), dma((2, 2)), dma((2, 2)), dma((4, CHUNKS, 2)), dma((4, CHUNKS, 2)),
        dma((2, n)), dma((2, n)), dma((4, n)), dma((4, n)), dma((3,)),
    ]
    any_spec = pl.BlockSpec(memory_space=pl.ANY)
    vmem_spec = pl.BlockSpec(memory_space=pltpu.VMEM)
    smem_spec = pl.BlockSpec(memory_space=pltpu.SMEM)
    pressure, wavefield, sat_gradient = pl.pallas_call(
        functools.partial(kernel, n, ni, fy, fz, sy, nx, sz),
        out_shape=(
            jax.ShapeDtypeStruct((ni, fy, fz), F32),
            jax.ShapeDtypeStruct((flat, sz), F32),
            jax.ShapeDtypeStruct((ni, fy, fz), F32),
        ),
        in_specs=[any_spec] * 11 + [vmem_spec] * 6 + [smem_spec] * 2,
        out_specs=(any_spec,) * 3,
        scratch_shapes=scratch,
        compiler_params=pltpu.CompilerParams(
            collective_id=0, has_side_effects=True, vmem_limit_bytes=60 * 1024 * 1024
        ),
        cost_estimate=pl.CostEstimate(flops=200000000, bytes_accessed=14000000, transcendentals=200000),
    )(
        right_side, storage, trans_x, trans_y, trans_z, sat_logit, porosity,
        background.reshape(flat, sz), wave_prev.reshape(flat, sz), wave_now.reshape(flat, sz),
        data_residual.reshape(flat, sz),
        well_cells.reshape(1, -1), well_rates.reshape(1, -1),
        y_index.reshape(1, -1), y_frac.reshape(1, -1), z_index.reshape(1, -1), z_frac.reshape(1, -1),
        y_index, y_frac,
    )
    results = (pressure, wavefield, sat_gradient)
    pressure, wavefield, sat_gradient = pl.pallas_call(
        move_out,
        out_shape=tuple(jax.ShapeDtypeStruct(r.shape, F32) for r in results),
        in_specs=[any_spec] * 3,
        out_specs=(any_spec,) * 3,
        scratch_shapes=[vm(*r.shape) for r in results] + [dma((3, MOVES)), dma((3, MOVES))],
        compiler_params=pltpu.CompilerParams(vmem_limit_bytes=32 * 1024 * 1024),
    )(*results)
    return pressure, wavefield.reshape(sy, nx, sz), sat_gradient


def solution(mesh):
    cells = P(("grp", "sx"), None, None)
    waves = P(None, ("grp", "sx"), None)
    in_specs = (
        cells, cells, P("grp", None), cells, cells, P("grp"), P("grp"), cells, cells,
        P(), P(), P(), P(), waves, waves, waves, waves,
    )
    return jax.shard_map(
        functools.partial(per_device, mesh.shape["sx"]),
        mesh=mesh, in_specs=in_specs, out_specs=(cells, waves, cells), check_vma=False,
    )
```

```python
import functools

import jax
import jax.numpy as jnp
from jax import lax
from jax.experimental import pallas as pl
from jax.experimental.pallas import tpu as pltpu
from jax.sharding import PartitionSpec as P

courant = 0.25
transport = 2.0
velocity_ref = 22.5
mineral_bulk = 37.0
mineral_shear = 44.0
carbon_bulk = 0.08
brine_bulk = 2.5
mineral_density = 2.65
carbon_density = 0.7
brine_density = 1.03

F32 = jnp.float32
BF16 = jnp.bfloat16
NN = (((1,), (0,)), ((), ()))
NT = (((1,), (1,)), ((), ()))
CHUNKS = 4
ROWS = 64
PAD = 8
MOVES = 4


def split(value):
    high = value.astype(BF16)
    return high, (value - high.astype(F32)).astype(BF16)


def dot3(a_high, a_low, b_high, b_low, dims):
    def one(a, b):
        return lax.dot_general(a, b, dims, preferred_element_type=F32)

    return one(a_high, b_high) + (one(a_high, b_low) + one(a_low, b_high))


def perturb_and_slope(sat, por):
    solid = 1.0 - por
    frame = solid * solid * solid
    dry = mineral_bulk * frame
    shear = mineral_shear * frame
    biot = 1.0 - frame
    biot2 = biot * biot
    soft = sat * (1.0 / carbon_bulk) + (1.0 - sat) * (1.0 / brine_bulk)
    inv = 1.0 / (por * soft + solid * (1.0 / mineral_bulk) - dry * (1.0 / (mineral_bulk * mineral_bulk)))
    ratio = biot2 * inv
    total = dry + ratio + (4.0 / 3.0) * shear
    density = mineral_density * solid + por * (carbon_density * sat + brine_density * (1.0 - sat))
    inv_density = 1.0 / density
    change = total * inv_density * (1.0 / velocity_ref) - 1.0
    bulk_slope = -ratio * inv * por * (1.0 / carbon_bulk - 1.0 / brine_bulk)
    density_slope = por * (carbon_density - brine_density)
    slope = (bulk_slope - total * inv_density * density_slope) * inv_density * (1.0 / velocity_ref)
    return change, slope


def kernel(
    n, ni, fy, fz, sy, nx, sz,
    rs_h, st_h, tx_h, ty_h, tz_h, sl_h, po_h, bg_h, wp_h, wn_h, dr_h,
    cells, rates, yi_v, yf_v, zi_v, zf_v, yi_s, yf_s,
    pr_o, wf_o, sg_o,
    f, af, a2, src, st, tx, ty, tz, sl, po, chg, slope, pres, recv, depth, rest, ret,
    ua, ub, w5, w4, a5, a4, a3, l1, l2, mod, grad, gz, wsend, wrecv, red,
    wzh, wzl, wyh, wyl,
    loc, hs, hr, ws, wr, rs_s, rs_r, as_s, as_r, out_s,
):
    me = lax.axis_index("sx")
    yc = sy // CHUNKS
    hx = nx // 2

    def wave_rows(ref):
        return ref.at[pl.ds(nx, sy * nx), :]

    def inner(ref):
        return ref.at[:, pl.ds(PAD, fy), :]

    loads = [
        pltpu.make_async_copy(a, b, loc.at[k])
        for k, (a, b) in enumerate(
            [
                (rs_h, f.at[pl.ds(1, ni), pl.ds(PAD, fy), :]),
                (st_h, st),
                (tx_h, tx),
                (ty_h, inner(ty)),
                (tz_h, tz),
                (wn_h, wave_rows(ub)),
                (sl_h, sl),
                (po_h, po),
                (bg_h, mod),
                (wp_h, wave_rows(ua)),
                (dr_h, a5),
            ]
        )
    ]
    for copy in loads:
        copy.start()

    barrier = pltpu.get_barrier_semaphore()

    def greet(o, _):
        pl.semaphore_signal(
            barrier, inc=1, device_id={"sx": lax.rem(me + o, n)},
            device_id_type=pl.DeviceIdType.MESH,
        )
        return 0

    lax.fori_loop(1, n, greet, 0)

    def remote(s, d, ssem, rsem, target):
        return pltpu.make_async_remote_copy(
            src_ref=s, dst_ref=d, send_sem=ssem, recv_sem=rsem,
            device_id={"sx": target}, device_id_type=pl.DeviceIdType.MESH,
        )

    has_left = me > 0
    has_right = me < n - 1

    def plane_copy(e, way):
        ref = (f, af)[e]
        here, there = ((1, ni + 1), (ni, 0))[way]
        return remote(
            ref.at[here, pl.ds(PAD, fy), :], ref.at[there, pl.ds(PAD, fy), :],
            hs.at[e, way], hr.at[e, way], me + (-1, 1)[way],
        )

    def wave_copy(e, q, way):
        if e == 0:
            s, d = wsend.at[e, way, q, 0], wrecv.at[e, 1 - way, q, 0]
        else:
            s, d = wsend.at[e, way, q], wrecv.at[e, 1 - way, q]
        return remote(s, d, ws.at[e, q, way], wr.at[e, q, way], me + (-1, 1)[way])

    def start_pair(make):
        pl.when(has_left)(lambda: make(0).start())
        pl.when(has_right)(lambda: make(1).start())

    def recv_pair(make):
        pl.when(has_right)(lambda: make(0).wait_recv())
        pl.when(has_left)(lambda: make(1).wait_recv())

    def start_way(make, way):
        pl.when((has_left, has_right)[way])(lambda: make(way).start())

    def recv_side(make, side):
        pl.when((has_left, has_right)[side])(lambda: make(1 - side).wait_recv())

    def sent_pair(make):
        pl.when(has_left)(lambda: make(0).wait_send())
        pl.when(has_right)(lambda: make(1).wait_send())

    rim = jnp.zeros((ni + 2, PAD, fz), F32)
    for ref in (f, af):
        ref[:, 0:PAD, :] = rim
        ref[:, PAD + fy:, :] = rim
    ty[:, 0:PAD, :] = rim[:ni]
    ty[:, PAD + fy:, :] = rim[:ni]
    zero_rows = jnp.zeros((nx, sz), F32)
    for ref in (ua, ub, w5, w4):
        ref[0:nx, :] = zero_rows
        ref[(sy + 1) * nx:, :] = zero_rows

    def zero_edge(plane, side):
        blank = jnp.zeros((fy, fz), F32)
        f[plane, pl.ds(PAD, fy), :] = blank
        af[plane, pl.ds(PAD, fy), :] = blank
        wrecv[:, side] = jnp.zeros((4, CHUNKS, 2, yc, sz), F32)

    pl.when(me == 0)(lambda: zero_edge(0, 0))
    pl.when(me == n - 1)(lambda: zero_edge(ni + 1, 1))

    cell_row = lax.shift_right_logical(cells[...], fz.bit_length() - 1)
    cell_col = cells[...] & (fz - 1)
    wells = cells.shape[1]
    rate_cols = jnp.where(
        lax.broadcasted_iota(jnp.int32, (fz, wells), 0) == cell_col, rates[...], 0.0
    )
    loads[0].wait()

    def well_plane(i):
        first = (me * ni + i) * fy
        hit = jnp.where(
            lax.broadcasted_iota(jnp.int32, (fy, wells), 0) + first == cell_row, 1.0, 0.0
        ).astype(F32)
        plane = lax.dot_general(
            hit, rate_cols, NT, precision=lax.Precision.HIGHEST, preferred_element_type=F32
        )
        src[i] = plane
        f[i + 1, pl.ds(PAD, fy), :] = f[i + 1, pl.ds(PAD, fy), :] + plane

    well_plane(0)
    well_plane(ni - 1)
    pl.semaphore_wait(barrier, n - 1)
    start_pair(functools.partial(plane_copy, 0))

    def mid_wells(i, _):
        well_plane(i)
        return 0

    lax.fori_loop(1, ni - 1, mid_wells, 0)

    row = lax.broadcasted_iota(jnp.int32, (fz, sz), 0)
    zi = zi_v[...]
    zf = zf_v[...]
    wz = jnp.where(row == zi, 1.0 - zf, 0.0) + jnp.where((row == zi + 1) & (zi >= 0), zf, 0.0)
    wzh[...], wzl[...] = split(wz)
    row = lax.broadcasted_iota(jnp.int32, (n * ni, sy), 0)
    yi = yi_v[...]
    yf = yf_v[...]
    wy = jnp.where(row == yi, 1.0 - yf, 0.0) + jnp.where((row == yi + 1) & (yi >= 0), yf, 0.0)
    wyh[...], wyl[...] = split(wy)

    for k in (1, 2, 3, 4):
        loads[k].wait()

    col = lax.broadcasted_iota(jnp.int32, (ROWS, fz), 1)

    def flow_apply(ref, i, j0):
        ext = ref[i, pl.ds(j0, ROWS + 2 * PAD), :]
        v = ext[PAD:PAD + ROWS]
        face = ty[i - 1, pl.ds(j0, ROWS + 2 * PAD), :] * (
            ext - pltpu.roll(ext, ROWS + 2 * PAD - 1, 0)
        )
        along_j = (face - pltpu.roll(face, 1, 0))[PAD:PAD + ROWS]
        up = jnp.where(col == fz - 1, 0.0, pltpu.roll(v, fz - 1, 1))
        face_z = tz[i - 1, pl.ds(j0, ROWS), :] * (v - up)
        along_k = face_z - jnp.where(col == 0, 0.0, pltpu.roll(face_z, 1, 1))
        mid = pl.ds(j0 + PAD, ROWS)
        along_i = tx[pl.ds(j0, ROWS), :] * (2.0 * v - ref[i + 1, mid, :] - ref[i - 1, mid, :])
        return v, st[i - 1, pl.ds(j0, ROWS), :] * v + along_i + along_j + along_k

    def fold(value):
        return jnp.sum(value.reshape(-1, 8, fz), axis=0)

    def image_plane(i, acc):
        def body(c, acc):
            j0 = pl.multiple_of(c * ROWS, ROWS)
            v, image = flow_apply(f, i, j0)
            af[i, pl.ds(j0 + PAD, ROWS), :] = image
            return acc[0] + fold(v * v), acc[1] + fold(v * image)

        return lax.fori_loop(0, fy // ROWS, body, acc)

    def image2_plane(i, _):
        def body(c, _):
            j0 = pl.multiple_of(c * ROWS, ROWS)
            a2[i - 1, pl.ds(j0, ROWS), :] = flow_apply(af, i, j0)[1]
            return 0

        return lax.fori_loop(0, fy // ROWS, body, 0)

    blank = jnp.zeros((8, fz), F32)
    acc = lax.fori_loop(2, ni, image_plane, (blank, blank))
    recv_side(functools.partial(plane_copy, 0), 0)
    acc = image_plane(1, acc)
    start_way(functools.partial(plane_copy, 1), 0)
    recv_side(functools.partial(plane_copy, 0), 1)
    acc = image_plane(ni, acc)

    def red_copy(r, o):
        return remote(
            red.at[r, me], red.at[r, me], rs_s.at[r, o], rs_r.at[r, o], lax.rem(me + o, n)
        )

    def reduce_start(r, parts):
        rows = [jnp.sum(p, axis=0, keepdims=True) for p in parts]
        which = lax.broadcasted_iota(jnp.int32, (8, fz), 0)
        tile = jnp.zeros((8, fz), F32)
        for k, p in enumerate(rows):
            tile = jnp.where(which == k, p, tile)
        red[r, me] = tile

        def go(o, _):
            red_copy(r, o).start()
            return 0

        lax.fori_loop(1, n, go, 0)

    def reduce_end(r):
        def go(o, _):
            red_copy(r, o).wait_recv()
            return 0

        lax.fori_loop(1, n, go, 0)
        return jnp.sum(jnp.sum(red[r], axis=0), axis=1, keepdims=True)

    reduce_start(0, acc)
    start_way(functools.partial(plane_copy, 1), 1)
    lax.fori_loop(2, ni, image2_plane, 0)

    loads[5].wait()

    def first_edges(q, _):
        def body(t, _):
            for s in range(8):
                y = q * yc + t * 8 + s
                for way, x in ((0, 0), (1, nx - 1)):
                    line = ub[pl.ds(pl.multiple_of((y + 1) * nx, nx), nx), :][x:x + 1]
                    wsend[0, way, q, 0, pl.ds(t * 8 + s, 1), :] = line
            return 0

        lax.fori_loop(0, yc // 8, body, 0)
        start_pair(functools.partial(wave_copy, 0, q))
        return 0

    lax.fori_loop(0, CHUNKS, first_edges, 0)

    sums = reduce_end(0)
    norm0 = sums[0:1]
    curve0 = sums[1:2]
    alpha0 = norm0 / curve0

    def dots_plane(i, acc):
        def body(c, acc):
            j0 = pl.multiple_of(c * ROWS, ROWS)
            g = af[i + 1, pl.ds(j0 + PAD, ROWS), :]
            r1 = f[i + 1, pl.ds(j0 + PAD, ROWS), :] - alpha0 * g
            ar1 = g - alpha0 * a2[i, pl.ds(j0, ROWS), :]
            return acc[0] + fold(r1 * r1), acc[1] + fold(r1 * ar1), acc[2] + fold(r1 * g)

        return lax.fori_loop(0, fy // ROWS, body, acc)

    acc = lax.fori_loop(1, ni - 1, dots_plane, (blank, blank, blank))
    recv_side(functools.partial(plane_copy, 1), 0)
    image2_plane(1, 0)
    acc = dots_plane(0, acc)
    recv_side(functools.partial(plane_copy, 1), 1)
    image2_plane(ni, 0)
    acc = dots_plane(ni - 1, acc)
    reduce_start(1, acc)

    zcol = lax.broadcasted_iota(jnp.int32, (nx, sz), 1)
    xrow = lax.broadcasted_iota(jnp.int32, (nx, sz), 0)

    def laplace(ref, y, low, high):
        here = pl.multiple_of((y + 1) * nx, nx)
        c = ref[pl.ds(here, nx), :]
        total = ref[pl.ds(pl.multiple_of(y * nx, nx), nx), :]
        total = total + ref[pl.ds(pl.multiple_of((y + 2) * nx, nx), nx), :]
        total = total + jnp.where(xrow == 0, low, pltpu.roll(c, 1, 0))
        total = total + jnp.where(xrow == nx - 1, high, pltpu.roll(c, nx - 1, 0))
        total = total + jnp.where(zcol == 0, 0.0, pltpu.roll(c, 1, 1))
        total = total + jnp.where(zcol == sz - 1, 0.0, pltpu.roll(c, sz - 1, 1))
        return c, total - 6.0 * c

    def first_stencil(q, _):
        recv_pair(functools.partial(wave_copy, 0, q))

        def body(t, _):
            lines = pl.ds(pl.multiple_of(t * 8, 8), 8)
            low = wrecv[0, 0, q, 0, lines, :]
            high = wrecv[0, 1, q, 0, lines, :]
            for s in range(8):
                y = q * yc + t * 8 + s
                _, lap = laplace(ub, y, low[s:s + 1], high[s:s + 1])
                l1[pl.ds(pl.multiple_of(y * nx, nx), nx), :] = lap
            return 0

        lax.fori_loop(0, yc // 8, body, 0)
        return 0

    lax.fori_loop(0, CHUNKS, first_stencil, 0)
    for k in (6, 7, 8, 9, 10):
        loads[k].wait()
    sums = reduce_end(1)
    norm1 = sums[0:1]
    beta = norm1 / norm0
    curve1 = sums[1:2] + 2.0 * beta * sums[2:3] + beta * beta * curve0
    alpha1 = norm1 / curve1
    c1 = alpha0 + alpha1 * (1.0 + beta)
    c2 = -alpha1 * alpha0

    def change_copy(o, h):
        d = lax.rem(me + o, n)
        return remote(
            chg.at[:, pl.ds(pl.multiple_of(d * nx + h * hx, hx), hx), :],
            recv.at[h, pl.ds(pl.multiple_of(me * ni, ni), ni)],
            as_s.at[h, o], as_r.at[h, o], d,
        )

    def columns_of(d, h):
        j0 = pl.multiple_of(d * nx + h * hx, hx)
        at = pl.ds(j0, hx)
        mid = pl.ds(pl.multiple_of(j0 + PAD, 8), hx)
        v = f[pl.ds(1, ni), mid, :]
        g = af[pl.ds(1, ni), mid, :]
        p = c1[0] * v + c2[0] * g
        ap = c1[0] * g + c2[0] * a2[:, at, :]
        inflow = st[:, at, :] * p - ap + src[:, at, :]
        sat = jax.nn.sigmoid(sl[:, at, :] + transport * inflow)
        value, gain = perturb_and_slope(sat, po[:, at, :])
        pres[:, at, :] = p
        slope[:, at, :] = gain
        return at, value

    def order(t):
        return 1 + lax.rem(t + n // 2 - 1, n - 1)

    for h in (0, 1):

        def send_change(t, _):
            o = order(t)
            at, value = columns_of(lax.rem(me + o, n), h)
            chg[:, at, :] = value
            change_copy(o, h).start()
            return 0

        lax.fori_loop(0, n - 1, send_change, 0)
    for h in (0, 1):
        _, value = columns_of(me, h)
        recv[h, pl.ds(pl.multiple_of(me * ni, ni), ni)] = value
    out_p = pltpu.make_async_copy(pres, pr_o, out_s.at[0])
    out_p.start()

    group = n * ni // 2

    def first_step(h):
        def take_change(t, _):
            change_copy(order(t), h).wait_recv()
            return 0

        lax.fori_loop(0, n - 1, take_change, 0)

        def blend_z(b, _):
            at = pl.ds(pl.multiple_of(b * group, group), group)
            high, low = split(recv[h, at].reshape(group * hx, fz))
            depth[h, at] = dot3(high, low, wzh[...], wzl[...], NN).reshape(group, hx, sz)
            return 0

        lax.fori_loop(0, 2, blend_z, 0)
        x = (0, hx - 1)[h]

        def chunk(q, _):
            def body(t, _):
                for s in range(8):
                    line = t * 8 + s
                    y = q * yc + line
                    at = pl.ds(pl.multiple_of(y * nx + h * hx, hx), hx)
                    pad_at = pl.ds(pl.multiple_of((y + 1) * nx + h * hx, hx), hx)
                    index = yi_s[y]
                    frac = yf_s[y]
                    lower_w = jnp.where(index >= 0, 1.0 - frac, 0.0)
                    upper_w = jnp.where(index >= 0, frac, 0.0)
                    base = jnp.maximum(index, 0)
                    lower = depth[h, base]
                    upper = depth[h, base + 1]
                    m = mod[at, :] + (lower_w * lower + upper_w * upper)
                    mod[at, :] = m
                    new = 2.0 * ub[pad_at, :] - ua[pad_at, :] + courant * m * l1[at, :]
                    w = m * a5[at, :]
                    ua[pad_at, :] = new
                    w5[pad_at, :] = w
                    wsend[1, h, q, 0, pl.ds(line, 1), :] = new[x:x + 1]
                    wsend[1, h, q, 1, pl.ds(line, 1), :] = w[x:x + 1]
                return 0

            lax.fori_loop(0, yc // 8, body, 0)
            start_way(functools.partial(wave_copy, 1, q), h)
            return 0

        lax.fori_loop(0, CHUNKS, chunk, 0)

    first_step(0)
    first_step(1)

    def middle_step(number):
        cur, old = ((ub, ua), (ua, ub))[(number - 1) % 2]
        w_in, w_out = ((w5, w4), (w4, w5))[number - 2]
        e = number - 1

        def chunk(q, _):
            recv_pair(functools.partial(wave_copy, e, q))

            def body(t, _):
                lines = pl.ds(pl.multiple_of(t * 8, 8), 8)
                edges = [
                    wrecv[e, side, q, what, lines, :] for what in range(2) for side in (0, 1)
                ]
                for s in range(8):
                    line = t * 8 + s
                    y = q * yc + line
                    at = pl.ds(pl.multiple_of(y * nx, nx), nx)
                    pad_at = pl.ds(pl.multiple_of((y + 1) * nx, nx), nx)
                    m = mod[at, :]
                    c, lap = laplace(cur, y, edges[0][s:s + 1], edges[1][s:s + 1])
                    new = 2.0 * c - old[pad_at, :] + courant * m * lap
                    _, lap_w = laplace(w_in, y, edges[2][s:s + 1], edges[3][s:s + 1])
                    if number == 2:
                        adj = 2.0 * a5[at, :] + courant * lap_w
                        a4[at, :] = adj
                        l2[at, :] = lap
                    else:
                        late = a4[at, :]
                        adj = 2.0 * late + courant * lap_w - a5[at, :]
                        a3[at, :] = adj
                        l2[at, :] = l2[at, :] * adj + lap * late
                    w = m * adj
                    old[pad_at, :] = new
                    w_out[pad_at, :] = w
                    for way, x in ((0, 0), (1, nx - 1)):
                        wsend[e + 1, way, q, 0, pl.ds(line, 1), :] = new[x:x + 1]
                        wsend[e + 1, way, q, 1, pl.ds(line, 1), :] = w[x:x + 1]
                return 0

            lax.fori_loop(0, yc // 8, body, 0)
            start_pair(functools.partial(wave_copy, e + 1, q))
            return 0

        lax.fori_loop(0, CHUNKS, chunk, 0)

    middle_step(2)
    middle_step(3)

    hcol = lax.broadcasted_iota(jnp.int32, (hx, sz), 1)
    hrow = lax.broadcasted_iota(jnp.int32, (hx, sz), 0)

    def half_laplace(ref, y, h, edge):
        def part(row, g):
            return ref[pl.ds(pl.multiple_of(row * nx + g * hx, hx), hx), :]

        c = part(y + 1, h)
        other = part(y + 1, 1 - h)
        low, high = ((edge, other[0:1]), (other[hx - 1:hx], edge))[h]
        total = part(y, h) + part(y + 2, h)
        total = total + jnp.where(hrow == 0, low, pltpu.roll(c, 1, 0))
        total = total + jnp.where(hrow == hx - 1, high, pltpu.roll(c, hx - 1, 0))
        total = total + jnp.where(hcol == 0, 0.0, pltpu.roll(c, 1, 1))
        total = total + jnp.where(hcol == sz - 1, 0.0, pltpu.roll(c, sz - 1, 1))
        return total - 6.0 * c

    def back_copy(o, h):
        d = lax.rem(me + o, n)
        size = ni * hx
        return remote(
            rest.at[h, pl.ds(pl.multiple_of(d * size, size), size), :],
            ret.at[h, me], as_s.at[2 + h, o], as_r.at[2 + h, o], d,
        )

    def last_step(h):
        def chunk(q, _):
            recv_side(functools.partial(wave_copy, 3, q), h)

            def body(t, _):
                lines = pl.ds(pl.multiple_of(t * 8, 8), 8)
                edge_u = wrecv[3, h, q, 0, lines, :]
                edge_w = wrecv[3, h, q, 1, lines, :]
                for s in range(8):
                    y = q * yc + t * 8 + s
                    at = pl.ds(pl.multiple_of(y * nx + h * hx, hx), hx)
                    lap = half_laplace(ua, y, h, edge_u[s:s + 1])
                    lap_w = half_laplace(w5, y, h, edge_w[s:s + 1])
                    adj = 2.0 * a3[at, :] + courant * lap_w - a4[at, :]
                    grad[h, pl.ds(pl.multiple_of(y * hx, hx), hx), :] = courant * (
                        l1[at, :] * adj + l2[at, :] + lap * a5[at, :]
                    )
                    l2[at, :] = lap
                return 0

            lax.fori_loop(0, yc // 8, body, 0)
            rows = pl.ds(pl.multiple_of(q * yc * hx, yc * hx), yc * hx)
            high, low = split(grad[h, rows, :])
            gz[h, rows, :] = dot3(high, low, wzh[...], wzl[...], NT)
            return 0

        lax.fori_loop(0, CHUNKS, chunk, 0)

        for x in range(hx):
            high, low = split(gz[h, pl.ds(x, sy, stride=hx), :])
            rest[h, pl.ds(x, n * ni, stride=hx), :] = dot3(wyh[...], wyl[...], high, low, NN)

        def send_back(t, _):
            back_copy(order(t), h).start()
            return 0

        lax.fori_loop(0, n - 1, send_back, 0)

    last_step(0)
    last_step(1)

    def last_wave(t, _):
        rows = 8 * nx
        at = pl.ds(pl.multiple_of(t * rows, rows), rows)
        pad_at = pl.ds(pl.multiple_of(t * rows + nx, nx), rows)
        ub[pad_at, :] = 2.0 * ua[pad_at, :] - ub[pad_at, :] + courant * mod[at, :] * l2[at, :]
        return 0

    lax.fori_loop(0, sy // 8, last_wave, 0)
    out_w = pltpu.make_async_copy(wave_rows(ub), wf_o, out_s.at[1])
    out_w.start()

    def finish(s, h, block):
        at = pl.ds(pl.multiple_of(s * nx + h * hx, hx), hx)
        slope[:, at, :] = slope[:, at, :] * block.reshape(ni, hx, fz)

    for h in (0, 1):
        size = ni * hx
        finish(me, h, rest[h, pl.ds(pl.multiple_of(me * size, size), size), :])

        def take_back(t, _):
            o = order(t)
            back_copy(o, h).wait_recv()
            s = lax.rem(me - o + n, n)
            finish(s, h, ret[h, s])
            return 0

        lax.fori_loop(0, n - 1, take_back, 0)
    out_g = pltpu.make_async_copy(slope, sg_o, out_s.at[2])
    out_g.start()

    for e in range(2):
        sent_pair(functools.partial(plane_copy, e))

    def sent_waves(q, _):
        for e in range(4):
            sent_pair(functools.partial(wave_copy, e, q))
        return 0

    lax.fori_loop(0, CHUNKS, sent_waves, 0)

    def sent_all(o, _):
        red_copy(0, o).wait_send()
        red_copy(1, o).wait_send()
        for h in (0, 1):
            change_copy(o, h).wait_send()
            back_copy(o, h).wait_send()
        return 0

    lax.fori_loop(1, n, sent_all, 0)
    out_p.wait()
    out_w.wait()
    out_g.wait()


def move_out(*refs):
    ins, outs, held, arrive, leave = refs[:3], refs[3:6], refs[6:9], refs[9], refs[10]
    moves = []
    for k in range(3):
        for part in range(MOVES):
            rows = ins[k].shape[0] // MOVES
            at = pl.ds(part * rows, rows)
            moves.append(
                (
                    pltpu.make_async_copy(ins[k].at[at], held[k].at[at], arrive.at[k, part]),
                    pltpu.make_async_copy(held[k].at[at], outs[k].at[at], leave.at[k, part]),
                )
            )
    for come, _ in moves:
        come.start()
    for come, go in moves:
        come.wait()
        go.start()
    for _, go in moves:
        go.wait()


def per_device(
    n, right_side, storage, trans_x, trans_y, trans_z, well_cells, well_rates, sat_logit, porosity,
    y_index, y_frac, z_index, z_frac, background, wave_prev, wave_now, data_residual,
):
    ni, fy, fz = right_side.shape
    sy, nx, sz = background.shape
    cells = ni * n
    flat = sy * nx

    def vm(*shape, dtype=F32):
        return pltpu.VMEM(shape, dtype)

    wide = (sy + 2) * nx
    scratch = [
        vm(ni + 2, fy + 2 * PAD, fz), vm(ni + 2, fy + 2 * PAD, fz), vm(ni, fy, fz), vm(ni, fy, fz),
        vm(ni, fy, fz), vm(fy, fz), vm(ni, fy + 2 * PAD, fz), vm(ni, fy, fz), vm(ni, fy, fz),
        vm(ni, fy, fz), vm(ni, fy, fz), vm(ni, fy, fz), vm(ni, fy, fz),
        vm(2, cells, nx // 2, fz), vm(2, cells, nx // 2, sz), vm(2, cells * nx // 2, fz),
        vm(2, n, ni * nx // 2, fz),
        vm(wide, sz), vm(wide, sz), vm(wide, sz), vm(wide, sz),
        vm(flat, sz), vm(flat, sz), vm(flat, sz), vm(flat, sz), vm(flat, sz), vm(flat, sz),
        vm(2, flat // 2, sz), vm(2, flat // 2, fz),
        vm(4, 2, CHUNKS, 2, sy // CHUNKS, sz), vm(4, 2, CHUNKS, 2, sy // CHUNKS, sz),
        vm(2, n, 8, fz),
        vm(fz, sz, dtype=BF16), vm(fz, sz, dtype=BF16), vm(cells, sy, dtype=BF16), vm(cells, sy, dtype=BF16),
    ]
    dma = pltpu.SemaphoreType.DMA
    scratch += [
        dma((11,)), dma((2, 2)), dma((2, 2)), dma((4, CHUNKS, 2)), dma((4, CHUNKS, 2)),
        dma((2, n)), dma((2, n)), dma((4, n)), dma((4, n)), dma((3,)),
    ]
    any_spec = pl.BlockSpec(memory_space=pl.ANY)
    vmem_spec = pl.BlockSpec(memory_space=pltpu.VMEM)
    smem_spec = pl.BlockSpec(memory_space=pltpu.SMEM)
    pressure, wavefield, sat_gradient = pl.pallas_call(
        functools.partial(kernel, n, ni, fy, fz, sy, nx, sz),
        out_shape=(
            jax.ShapeDtypeStruct((ni, fy, fz), F32),
            jax.ShapeDtypeStruct((flat, sz), F32),
            jax.ShapeDtypeStruct((ni, fy, fz), F32),
        ),
        in_specs=[any_spec] * 11 + [vmem_spec] * 6 + [smem_spec] * 2,
        out_specs=(any_spec,) * 3,
        scratch_shapes=scratch,
        compiler_params=pltpu.CompilerParams(
            collective_id=0, has_side_effects=True, vmem_limit_bytes=60 * 1024 * 1024
        ),
        cost_estimate=pl.CostEstimate(flops=200000000, bytes_accessed=14000000, transcendentals=200000),
    )(
        right_side, storage, trans_x, trans_y, trans_z, sat_logit, porosity,
        background.reshape(flat, sz), wave_prev.reshape(flat, sz), wave_now.reshape(flat, sz),
        data_residual.reshape(flat, sz),
        well_cells.reshape(1, -1), well_rates.reshape(1, -1),
        y_index.reshape(1, -1), y_frac.reshape(1, -1), z_index.reshape(1, -1), z_frac.reshape(1, -1),
        y_index, y_frac,
    )
    results = (pressure, wavefield, sat_gradient)
    pressure, wavefield, sat_gradient = pl.pallas_call(
        move_out,
        out_shape=tuple(jax.ShapeDtypeStruct(r.shape, F32) for r in results),
        in_specs=[any_spec] * 3,
        out_specs=(any_spec,) * 3,
        scratch_shapes=[vm(*r.shape) for r in results] + [dma((3, MOVES)), dma((3, MOVES))],
        compiler_params=pltpu.CompilerParams(vmem_limit_bytes=60 * 1024 * 1024),
    )(*results)
    return pressure, wavefield.reshape(sy, nx, sz), sat_gradient


def solution(mesh):
    cells = P(("grp", "sx"), None, None)
    waves = P(None, ("grp", "sx"), None)
    in_specs = (
        cells, cells, P("grp", None), cells, cells, P("grp"), P("grp"), cells, cells,
        P(), P(), P(), P(), waves, waves, waves, waves,
    )
    return jax.shard_map(
        functools.partial(per_device, mesh.shape["sx"]),
        mesh=mesh, in_specs=in_specs, out_specs=(cells, waves, cells), check_vma=False,
    )
```

```python
import functools

import jax
import jax.numpy as jnp
from jax import lax
from jax.experimental import pallas as pl
from jax.experimental.pallas import tpu as pltpu
from jax.sharding import PartitionSpec as P

courant = 0.25
transport = 2.0
velocity_ref = 22.5
mineral_bulk = 37.0
mineral_shear = 44.0
carbon_bulk = 0.08
brine_bulk = 2.5
mineral_density = 2.65
carbon_density = 0.7
brine_density = 1.03

F32 = jnp.float32
BF16 = jnp.bfloat16
NN = (((1,), (0,)), ((), ()))
NT = (((1,), (1,)), ((), ()))
CHUNKS = 4
ROWS = 64
PAD = 8
MOVES = 4


def split(value):
    high = value.astype(BF16)
    return high, (value - high.astype(F32)).astype(BF16)


def dot3(a_high, a_low, b_high, b_low, dims):
    def one(a, b):
        return lax.dot_general(a, b, dims, preferred_element_type=F32)

    return one(a_high, b_high) + (one(a_high, b_low) + one(a_low, b_high))


def perturb_and_slope(sat, por):
    solid = 1.0 - por
    frame = solid * solid * solid
    dry = mineral_bulk * frame
    shear = mineral_shear * frame
    biot = 1.0 - frame
    biot2 = biot * biot
    soft = sat * (1.0 / carbon_bulk) + (1.0 - sat) * (1.0 / brine_bulk)
    inv = 1.0 / (por * soft + solid * (1.0 / mineral_bulk) - dry * (1.0 / (mineral_bulk * mineral_bulk)))
    ratio = biot2 * inv
    total = dry + ratio + (4.0 / 3.0) * shear
    density = mineral_density * solid + por * (carbon_density * sat + brine_density * (1.0 - sat))
    inv_density = 1.0 / density
    change = total * inv_density * (1.0 / velocity_ref) - 1.0
    bulk_slope = -ratio * inv * por * (1.0 / carbon_bulk - 1.0 / brine_bulk)
    density_slope = por * (carbon_density - brine_density)
    slope = (bulk_slope - total * inv_density * density_slope) * inv_density * (1.0 / velocity_ref)
    return change, slope


def kernel(
    n, ni, fy, fz, sy, nx, sz,
    rs_h, st_h, tx_h, ty_h, tz_h, sl_h, po_h, bg_h, wp_h, wn_h, dr_h,
    cells, rates, yi_v, yf_v, zi_v, zf_v, yi_s, yf_s,
    pr_o, wf_o, sg_o,
    f, af, a2, src, st, tx, ty, tz, sl, po, chg, slope, pres, recv, depth, rest, ret,
    ua, ub, w5, w4, a5, a4, a3, l1, l2, mod, grad, gz, wsend, wrecv, red,
    wzh, wzl, wyh, wyl,
    loc, hs, hr, ws, wr, rs_s, rs_r, as_s, as_r, out_s,
):
    me = lax.axis_index("sx")
    yc = sy // CHUNKS
    hx = nx // 2

    def wave_rows(ref):
        return ref.at[pl.ds(nx, sy * nx), :]

    def inner(ref):
        return ref.at[:, pl.ds(PAD, fy), :]

    loads = [
        pltpu.make_async_copy(a, b, loc.at[k])
        for k, (a, b) in enumerate(
            [
                (rs_h, f.at[pl.ds(1, ni), pl.ds(PAD, fy), :]),
                (st_h, st),
                (tx_h, tx),
                (ty_h, inner(ty)),
                (tz_h, tz),
                (wn_h, wave_rows(ub)),
                (sl_h, sl),
                (po_h, po),
                (bg_h, mod),
                (wp_h, wave_rows(ua)),
                (dr_h, a5),
            ]
        )
    ]
    for copy in loads:
        copy.start()

    barrier = pltpu.get_barrier_semaphore()

    def greet(o, _):
        pl.semaphore_signal(
            barrier, inc=1, device_id={"sx": lax.rem(me + o, n)},
            device_id_type=pl.DeviceIdType.MESH,
        )
        return 0

    lax.fori_loop(1, n, greet, 0)

    def remote(s, d, ssem, rsem, target):
        return pltpu.make_async_remote_copy(
            src_ref=s, dst_ref=d, send_sem=ssem, recv_sem=rsem,
            device_id={"sx": target}, device_id_type=pl.DeviceIdType.MESH,
        )

    has_left = me > 0
    has_right = me < n - 1

    def plane_copy(e, way):
        ref = (f, af)[e]
        here, there = ((1, ni + 1), (ni, 0))[way]
        return remote(
            ref.at[here, pl.ds(PAD, fy), :], ref.at[there, pl.ds(PAD, fy), :],
            hs.at[e, way], hr.at[e, way], me + (-1, 1)[way],
        )

    def wave_copy(e, q, way):
        if e == 0:
            s, d = wsend.at[e, way, q, 0], wrecv.at[e, 1 - way, q, 0]
        else:
            s, d = wsend.at[e, way, q], wrecv.at[e, 1 - way, q]
        return remote(s, d, ws.at[e, q, way], wr.at[e, q, way], me + (-1, 1)[way])

    def start_pair(make):
        pl.when(has_left)(lambda: make(0).start())
        pl.when(has_right)(lambda: make(1).start())

    def recv_pair(make):
        pl.when(has_right)(lambda: make(0).wait_recv())
        pl.when(has_left)(lambda: make(1).wait_recv())

    def start_way(make, way):
        pl.when((has_left, has_right)[way])(lambda: make(way).start())

    def recv_side(make, side):
        pl.when((has_left, has_right)[side])(lambda: make(1 - side).wait_recv())

    def sent_pair(make):
        pl.when(has_left)(lambda: make(0).wait_send())
        pl.when(has_right)(lambda: make(1).wait_send())

    rim = jnp.zeros((ni + 2, PAD, fz), F32)
    for ref in (f, af):
        ref[:, 0:PAD, :] = rim
        ref[:, PAD + fy:, :] = rim
    ty[:, 0:PAD, :] = rim[:ni]
    ty[:, PAD + fy:, :] = rim[:ni]
    zero_rows = jnp.zeros((nx, sz), F32)
    for ref in (ua, ub, w5, w4):
        ref[0:nx, :] = zero_rows
        ref[(sy + 1) * nx:, :] = zero_rows

    def zero_edge(plane, side):
        blank = jnp.zeros((fy, fz), F32)
        f[plane, pl.ds(PAD, fy), :] = blank
        af[plane, pl.ds(PAD, fy), :] = blank
        wrecv[:, side] = jnp.zeros((4, CHUNKS, 2, yc, sz), F32)

    pl.when(me == 0)(lambda: zero_edge(0, 0))
    pl.when(me == n - 1)(lambda: zero_edge(ni + 1, 1))

    cell_row = lax.shift_right_logical(cells[...], fz.bit_length() - 1)
    cell_col = cells[...] & (fz - 1)
    wells = cells.shape[1]
    rate_cols = jnp.where(
        lax.broadcasted_iota(jnp.int32, (fz, wells), 0) == cell_col, rates[...], 0.0
    )
    loads[0].wait()

    def well_plane(i):
        first = (me * ni + i) * fy
        hit = jnp.where(
            lax.broadcasted_iota(jnp.int32, (fy, wells), 0) + first == cell_row, 1.0, 0.0
        ).astype(F32)
        plane = lax.dot_general(
            hit, rate_cols, NT, precision=lax.Precision.HIGHEST, preferred_element_type=F32
        )
        src[i] = plane
        f[i + 1, pl.ds(PAD, fy), :] = f[i + 1, pl.ds(PAD, fy), :] + plane

    well_plane(0)
    well_plane(ni - 1)
    pl.semaphore_wait(barrier, n - 1)
    start_pair(functools.partial(plane_copy, 0))

    def mid_wells(i, _):
        well_plane(i)
        return 0

    lax.fori_loop(1, ni - 1, mid_wells, 0)

    row = lax.broadcasted_iota(jnp.int32, (fz, sz), 0)
    zi = zi_v[...]
    zf = zf_v[...]
    wz = jnp.where(row == zi, 1.0 - zf, 0.0) + jnp.where((row == zi + 1) & (zi >= 0), zf, 0.0)
    wzh[...], wzl[...] = split(wz)
    row = lax.broadcasted_iota(jnp.int32, (n * ni, sy), 0)
    yi = yi_v[...]
    yf = yf_v[...]
    wy = jnp.where(row == yi, 1.0 - yf, 0.0) + jnp.where((row == yi + 1) & (yi >= 0), yf, 0.0)
    wyh[...], wyl[...] = split(wy)

    for k in (1, 2, 3, 4):
        loads[k].wait()

    col = lax.broadcasted_iota(jnp.int32, (ROWS, fz), 1)

    def flow_apply(ref, i, j0):
        ext = ref[i, pl.ds(j0, ROWS + 2 * PAD), :]
        v = ext[PAD:PAD + ROWS]
        face = ty[i - 1, pl.ds(j0, ROWS + 2 * PAD), :] * (
            ext - pltpu.roll(ext, ROWS + 2 * PAD - 1, 0)
        )
        along_j = (face - pltpu.roll(face, 1, 0))[PAD:PAD + ROWS]
        up = jnp.where(col == fz - 1, 0.0, pltpu.roll(v, fz - 1, 1))
        face_z = tz[i - 1, pl.ds(j0, ROWS), :] * (v - up)
        along_k = face_z - jnp.where(col == 0, 0.0, pltpu.roll(face_z, 1, 1))
        mid = pl.ds(j0 + PAD, ROWS)
        along_i = tx[pl.ds(j0, ROWS), :] * (2.0 * v - ref[i + 1, mid, :] - ref[i - 1, mid, :])
        return v, st[i - 1, pl.ds(j0, ROWS), :] * v + along_i + along_j + along_k

    def fold(value):
        return jnp.sum(value.reshape(-1, 8, fz), axis=0)

    def image_plane(i, acc):
        def body(c, acc):
            j0 = pl.multiple_of(c * ROWS, ROWS)
            v, image = flow_apply(f, i, j0)
            af[i, pl.ds(j0 + PAD, ROWS), :] = image
            return acc[0] + fold(v * v), acc[1] + fold(v * image)

        return lax.fori_loop(0, fy // ROWS, body, acc)

    def image2_plane(i, _):
        def body(c, _):
            j0 = pl.multiple_of(c * ROWS, ROWS)
            a2[i - 1, pl.ds(j0, ROWS), :] = flow_apply(af, i, j0)[1]
            return 0

        return lax.fori_loop(0, fy // ROWS, body, 0)

    blank = jnp.zeros((8, fz), F32)
    acc = lax.fori_loop(2, ni, image_plane, (blank, blank))
    recv_side(functools.partial(plane_copy, 0), 0)
    acc = image_plane(1, acc)
    start_way(functools.partial(plane_copy, 1), 0)
    recv_side(functools.partial(plane_copy, 0), 1)
    acc = image_plane(ni, acc)

    def red_copy(r, o):
        return remote(
            red.at[r, me], red.at[r, me], rs_s.at[r, o], rs_r.at[r, o], lax.rem(me + o, n)
        )

    def reduce_start(r, parts):
        rows = [jnp.sum(p, axis=0, keepdims=True) for p in parts]
        which = lax.broadcasted_iota(jnp.int32, (8, fz), 0)
        tile = jnp.zeros((8, fz), F32)
        for k, p in enumerate(rows):
            tile = jnp.where(which == k, p, tile)
        red[r, me] = tile

        def go(o, _):
            red_copy(r, o).start()
            return 0

        lax.fori_loop(1, n, go, 0)

    def reduce_end(r):
        def go(o, _):
            red_copy(r, o).wait_recv()
            return 0

        lax.fori_loop(1, n, go, 0)
        return jnp.sum(jnp.sum(red[r], axis=0), axis=1, keepdims=True)

    reduce_start(0, acc)
    start_way(functools.partial(plane_copy, 1), 1)
    lax.fori_loop(2, ni, image2_plane, 0)

    loads[5].wait()

    def first_edges(q, _):
        def body(t, _):
            for s in range(8):
                y = q * yc + t * 8 + s
                for way, x in ((0, 0), (1, nx - 1)):
                    line = ub[pl.ds(pl.multiple_of((y + 1) * nx, nx), nx), :][x:x + 1]
                    wsend[0, way, q, 0, pl.ds(t * 8 + s, 1), :] = line
            return 0

        lax.fori_loop(0, yc // 8, body, 0)
        start_pair(functools.partial(wave_copy, 0, q))
        return 0

    lax.fori_loop(0, CHUNKS, first_edges, 0)

    sums = reduce_end(0)
    norm0 = sums[0:1]
    curve0 = sums[1:2]
    alpha0 = norm0 / curve0

    def dots_plane(i, acc):
        def body(c, acc):
            j0 = pl.multiple_of(c * ROWS, ROWS)
            g = af[i + 1, pl.ds(j0 + PAD, ROWS), :]
            r1 = f[i + 1, pl.ds(j0 + PAD, ROWS), :] - alpha0 * g
            ar1 = g - alpha0 * a2[i, pl.ds(j0, ROWS), :]
            return acc[0] + fold(r1 * r1), acc[1] + fold(r1 * ar1), acc[2] + fold(r1 * g)

        return lax.fori_loop(0, fy // ROWS, body, acc)

    acc = lax.fori_loop(1, ni - 1, dots_plane, (blank, blank, blank))
    recv_side(functools.partial(plane_copy, 1), 0)
    image2_plane(1, 0)
    acc = dots_plane(0, acc)
    recv_side(functools.partial(plane_copy, 1), 1)
    image2_plane(ni, 0)
    acc = dots_plane(ni - 1, acc)
    reduce_start(1, acc)

    zcol = lax.broadcasted_iota(jnp.int32, (nx, sz), 1)
    xrow = lax.broadcasted_iota(jnp.int32, (nx, sz), 0)

    def laplace(ref, y, low, high):
        here = pl.multiple_of((y + 1) * nx, nx)
        c = ref[pl.ds(here, nx), :]
        total = ref[pl.ds(pl.multiple_of(y * nx, nx), nx), :]
        total = total + ref[pl.ds(pl.multiple_of((y + 2) * nx, nx), nx), :]
        total = total + jnp.where(xrow == 0, low, pltpu.roll(c, 1, 0))
        total = total + jnp.where(xrow == nx - 1, high, pltpu.roll(c, nx - 1, 0))
        total = total + jnp.where(zcol == 0, 0.0, pltpu.roll(c, 1, 1))
        total = total + jnp.where(zcol == sz - 1, 0.0, pltpu.roll(c, sz - 1, 1))
        return c, total - 6.0 * c

    def first_stencil(q, _):
        recv_pair(functools.partial(wave_copy, 0, q))

        def body(t, _):
            lines = pl.ds(pl.multiple_of(t * 8, 8), 8)
            low = wrecv[0, 0, q, 0, lines, :]
            high = wrecv[0, 1, q, 0, lines, :]
            for s in range(8):
                y = q * yc + t * 8 + s
                _, lap = laplace(ub, y, low[s:s + 1], high[s:s + 1])
                l1[pl.ds(pl.multiple_of(y * nx, nx), nx), :] = lap
            return 0

        lax.fori_loop(0, yc // 8, body, 0)
        return 0

    lax.fori_loop(0, CHUNKS, first_stencil, 0)
    for k in (6, 7, 8, 9, 10):
        loads[k].wait()
    sums = reduce_end(1)
    norm1 = sums[0:1]
    beta = norm1 / norm0
    curve1 = sums[1:2] + 2.0 * beta * sums[2:3] + beta * beta * curve0
    alpha1 = norm1 / curve1
    c1 = alpha0 + alpha1 * (1.0 + beta)
    c2 = -alpha1 * alpha0

    def change_copy(o, h):
        d = lax.rem(me + o, n)
        return remote(
            chg.at[:, pl.ds(pl.multiple_of(d * nx + h * hx, hx), hx), :],
            recv.at[h, pl.ds(pl.multiple_of(me * ni, ni), ni)],
            as_s.at[h, o], as_r.at[h, o], d,
        )

    def columns_of(d, h):
        j0 = pl.multiple_of(d * nx + h * hx, hx)
        at = pl.ds(j0, hx)
        mid = pl.ds(pl.multiple_of(j0 + PAD, 8), hx)
        v = f[pl.ds(1, ni), mid, :]
        g = af[pl.ds(1, ni), mid, :]
        p = c1[0] * v + c2[0] * g
        ap = c1[0] * g + c2[0] * a2[:, at, :]
        inflow = st[:, at, :] * p - ap + src[:, at, :]
        sat = jax.nn.sigmoid(sl[:, at, :] + transport * inflow)
        value, gain = perturb_and_slope(sat, po[:, at, :])
        pres[:, at, :] = p
        slope[:, at, :] = gain
        return at, value

    def order(t):
        step = (t + 1) // 2
        return n // 2 + step * (1 - 2 * lax.rem(t + 1, 2))

    for h in (0, 1):

        def send_change(t, _):
            o = order(t)
            at, value = columns_of(lax.rem(me + o, n), h)
            chg[:, at, :] = value
            change_copy(o, h).start()
            return 0

        lax.fori_loop(0, n - 1, send_change, 0)
    for h in (0, 1):
        _, value = columns_of(me, h)
        recv[h, pl.ds(pl.multiple_of(me * ni, ni), ni)] = value
    out_p = pltpu.make_async_copy(pres, pr_o, out_s.at[0])
    out_p.start()

    group = n * ni // 2

    def first_step(h):
        def take_change(t, _):
            change_copy(order(t), h).wait_recv()
            return 0

        lax.fori_loop(0, n - 1, take_change, 0)

        def blend_z(b, _):
            at = pl.ds(pl.multiple_of(b * group, group), group)
            high, low = split(recv[h, at].reshape(group * hx, fz))
            depth[h, at] = dot3(high, low, wzh[...], wzl[...], NN).reshape(group, hx, sz)
            return 0

        lax.fori_loop(0, 2, blend_z, 0)
        x = (0, hx - 1)[h]

        def chunk(q, _):
            def body(t, _):
                for s in range(8):
                    line = t * 8 + s
                    y = q * yc + line
                    at = pl.ds(pl.multiple_of(y * nx + h * hx, hx), hx)
                    pad_at = pl.ds(pl.multiple_of((y + 1) * nx + h * hx, hx), hx)
                    index = yi_s[y]
                    frac = yf_s[y]
                    lower_w = jnp.where(index >= 0, 1.0 - frac, 0.0)
                    upper_w = jnp.where(index >= 0, frac, 0.0)
                    base = jnp.maximum(index, 0)
                    lower = depth[h, base]
                    upper = depth[h, base + 1]
                    m = mod[at, :] + (lower_w * lower + upper_w * upper)
                    mod[at, :] = m
                    new = 2.0 * ub[pad_at, :] - ua[pad_at, :] + courant * m * l1[at, :]
                    w = m * a5[at, :]
                    ua[pad_at, :] = new
                    w5[pad_at, :] = w
                    wsend[1, h, q, 0, pl.ds(line, 1), :] = new[x:x + 1]
                    wsend[1, h, q, 1, pl.ds(line, 1), :] = w[x:x + 1]
                return 0

            lax.fori_loop(0, yc // 8, body, 0)
            start_way(functools.partial(wave_copy, 1, q), h)
            return 0

        lax.fori_loop(0, CHUNKS, chunk, 0)

    first_step(0)
    first_step(1)

    def middle_step(number):
        cur, old = ((ub, ua), (ua, ub))[(number - 1) % 2]
        w_in, w_out = ((w5, w4), (w4, w5))[number - 2]
        e = number - 1

        def chunk(q, _):
            recv_pair(functools.partial(wave_copy, e, q))

            def body(t, _):
                lines = pl.ds(pl.multiple_of(t * 8, 8), 8)
                edges = [
                    wrecv[e, side, q, what, lines, :] for what in range(2) for side in (0, 1)
                ]
                for s in range(8):
                    line = t * 8 + s
                    y = q * yc + line
                    at = pl.ds(pl.multiple_of(y * nx, nx), nx)
                    pad_at = pl.ds(pl.multiple_of((y + 1) * nx, nx), nx)
                    m = mod[at, :]
                    c, lap = laplace(cur, y, edges[0][s:s + 1], edges[1][s:s + 1])
                    new = 2.0 * c - old[pad_at, :] + courant * m * lap
                    _, lap_w = laplace(w_in, y, edges[2][s:s + 1], edges[3][s:s + 1])
                    if number == 2:
                        adj = 2.0 * a5[at, :] + courant * lap_w
                        a4[at, :] = adj
                        l2[at, :] = lap
                    else:
                        late = a4[at, :]
                        adj = 2.0 * late + courant * lap_w - a5[at, :]
                        a3[at, :] = adj
                        l2[at, :] = l2[at, :] * adj + lap * late
                    w = m * adj
                    old[pad_at, :] = new
                    w_out[pad_at, :] = w
                    for way, x in ((0, 0), (1, nx - 1)):
                        wsend[e + 1, way, q, 0, pl.ds(line, 1), :] = new[x:x + 1]
                        wsend[e + 1, way, q, 1, pl.ds(line, 1), :] = w[x:x + 1]
                return 0

            lax.fori_loop(0, yc // 8, body, 0)
            start_pair(functools.partial(wave_copy, e + 1, q))
            return 0

        lax.fori_loop(0, CHUNKS, chunk, 0)

    middle_step(2)
    middle_step(3)

    hcol = lax.broadcasted_iota(jnp.int32, (hx, sz), 1)
    hrow = lax.broadcasted_iota(jnp.int32, (hx, sz), 0)

    def half_laplace(ref, y, h, edge):
        def part(row, g):
            return ref[pl.ds(pl.multiple_of(row * nx + g * hx, hx), hx), :]

        c = part(y + 1, h)
        other = part(y + 1, 1 - h)
        low, high = ((edge, other[0:1]), (other[hx - 1:hx], edge))[h]
        total = part(y, h) + part(y + 2, h)
        total = total + jnp.where(hrow == 0, low, pltpu.roll(c, 1, 0))
        total = total + jnp.where(hrow == hx - 1, high, pltpu.roll(c, hx - 1, 0))
        total = total + jnp.where(hcol == 0, 0.0, pltpu.roll(c, 1, 1))
        total = total + jnp.where(hcol == sz - 1, 0.0, pltpu.roll(c, sz - 1, 1))
        return total - 6.0 * c

    def back_copy(o, h):
        d = lax.rem(me + o, n)
        size = ni * hx
        return remote(
            rest.at[h, pl.ds(pl.multiple_of(d * size, size), size), :],
            ret.at[h, me], as_s.at[2 + h, o], as_r.at[2 + h, o], d,
        )

    def last_step(h):
        def chunk(q, _):
            recv_side(functools.partial(wave_copy, 3, q), h)

            def body(t, _):
                lines = pl.ds(pl.multiple_of(t * 8, 8), 8)
                edge_u = wrecv[3, h, q, 0, lines, :]
                edge_w = wrecv[3, h, q, 1, lines, :]
                for s in range(8):
                    y = q * yc + t * 8 + s
                    at = pl.ds(pl.multiple_of(y * nx + h * hx, hx), hx)
                    lap = half_laplace(ua, y, h, edge_u[s:s + 1])
                    lap_w = half_laplace(w5, y, h, edge_w[s:s + 1])
                    adj = 2.0 * a3[at, :] + courant * lap_w - a4[at, :]
                    grad[h, pl.ds(pl.multiple_of(y * hx, hx), hx), :] = courant * (
                        l1[at, :] * adj + l2[at, :] + lap * a5[at, :]
                    )
                    l2[at, :] = lap
                return 0

            lax.fori_loop(0, yc // 8, body, 0)
            rows = pl.ds(pl.multiple_of(q * yc * hx, yc * hx), yc * hx)
            high, low = split(grad[h, rows, :])
            gz[h, rows, :] = dot3(high, low, wzh[...], wzl[...], NT)
            return 0

        lax.fori_loop(0, CHUNKS, chunk, 0)

        for x in range(hx):
            high, low = split(gz[h, pl.ds(x, sy, stride=hx), :])
            rest[h, pl.ds(x, n * ni, stride=hx), :] = dot3(wyh[...], wyl[...], high, low, NN)

        def send_back(t, _):
            back_copy(order(t), h).start()
            return 0

        lax.fori_loop(0, n - 1, send_back, 0)

    last_step(0)
    last_step(1)

    def last_wave(t, _):
        rows = 8 * nx
        at = pl.ds(pl.multiple_of(t * rows, rows), rows)
        pad_at = pl.ds(pl.multiple_of(t * rows + nx, nx), rows)
        ub[pad_at, :] = 2.0 * ua[pad_at, :] - ub[pad_at, :] + courant * mod[at, :] * l2[at, :]
        return 0

    lax.fori_loop(0, sy // 8, last_wave, 0)
    out_w = pltpu.make_async_copy(wave_rows(ub), wf_o, out_s.at[1])
    out_w.start()

    def finish(s, h, block):
        at = pl.ds(pl.multiple_of(s * nx + h * hx, hx), hx)
        slope[:, at, :] = slope[:, at, :] * block.reshape(ni, hx, fz)

    for h in (0, 1):
        size = ni * hx
        finish(me, h, rest[h, pl.ds(pl.multiple_of(me * size, size), size), :])

        def take_back(t, _):
            o = order(t)
            back_copy(o, h).wait_recv()
            s = lax.rem(me - o + n, n)
            finish(s, h, ret[h, s])
            return 0

        lax.fori_loop(0, n - 1, take_back, 0)
    out_g = pltpu.make_async_copy(slope, sg_o, out_s.at[2])
    out_g.start()

    for e in range(2):
        sent_pair(functools.partial(plane_copy, e))

    def sent_waves(q, _):
        for e in range(4):
            sent_pair(functools.partial(wave_copy, e, q))
        return 0

    lax.fori_loop(0, CHUNKS, sent_waves, 0)

    def sent_all(o, _):
        red_copy(0, o).wait_send()
        red_copy(1, o).wait_send()
        for h in (0, 1):
            change_copy(o, h).wait_send()
            back_copy(o, h).wait_send()
        return 0

    lax.fori_loop(1, n, sent_all, 0)
    out_p.wait()
    out_w.wait()
    out_g.wait()


def move_out(*refs):
    ins, outs, held, arrive, leave = refs[:3], refs[3:6], refs[6:9], refs[9], refs[10]
    moves = []
    for k in range(3):
        for part in range(MOVES):
            rows = ins[k].shape[0] // MOVES
            at = pl.ds(part * rows, rows)
            moves.append(
                (
                    pltpu.make_async_copy(ins[k].at[at], held[k].at[at], arrive.at[k, part]),
                    pltpu.make_async_copy(held[k].at[at], outs[k].at[at], leave.at[k, part]),
                )
            )
    for come, _ in moves:
        come.start()
    for come, go in moves:
        come.wait()
        go.start()
    for _, go in moves:
        go.wait()


def per_device(
    n, right_side, storage, trans_x, trans_y, trans_z, well_cells, well_rates, sat_logit, porosity,
    y_index, y_frac, z_index, z_frac, background, wave_prev, wave_now, data_residual,
):
    ni, fy, fz = right_side.shape
    sy, nx, sz = background.shape
    cells = ni * n
    flat = sy * nx

    def vm(*shape, dtype=F32):
        return pltpu.VMEM(shape, dtype)

    wide = (sy + 2) * nx
    scratch = [
        vm(ni + 2, fy + 2 * PAD, fz), vm(ni + 2, fy + 2 * PAD, fz), vm(ni, fy, fz), vm(ni, fy, fz),
        vm(ni, fy, fz), vm(fy, fz), vm(ni, fy + 2 * PAD, fz), vm(ni, fy, fz), vm(ni, fy, fz),
        vm(ni, fy, fz), vm(ni, fy, fz), vm(ni, fy, fz), vm(ni, fy, fz),
        vm(2, cells, nx // 2, fz), vm(2, cells, nx // 2, sz), vm(2, cells * nx // 2, fz),
        vm(2, n, ni * nx // 2, fz),
        vm(wide, sz), vm(wide, sz), vm(wide, sz), vm(wide, sz),
        vm(flat, sz), vm(flat, sz), vm(flat, sz), vm(flat, sz), vm(flat, sz), vm(flat, sz),
        vm(2, flat // 2, sz), vm(2, flat // 2, fz),
        vm(4, 2, CHUNKS, 2, sy // CHUNKS, sz), vm(4, 2, CHUNKS, 2, sy // CHUNKS, sz),
        vm(2, n, 8, fz),
        vm(fz, sz, dtype=BF16), vm(fz, sz, dtype=BF16), vm(cells, sy, dtype=BF16), vm(cells, sy, dtype=BF16),
    ]
    dma = pltpu.SemaphoreType.DMA
    scratch += [
        dma((11,)), dma((2, 2)), dma((2, 2)), dma((4, CHUNKS, 2)), dma((4, CHUNKS, 2)),
        dma((2, n)), dma((2, n)), dma((4, n)), dma((4, n)), dma((3,)),
    ]
    any_spec = pl.BlockSpec(memory_space=pl.ANY)
    vmem_spec = pl.BlockSpec(memory_space=pltpu.VMEM)
    smem_spec = pl.BlockSpec(memory_space=pltpu.SMEM)
    pressure, wavefield, sat_gradient = pl.pallas_call(
        functools.partial(kernel, n, ni, fy, fz, sy, nx, sz),
        out_shape=(
            jax.ShapeDtypeStruct((ni, fy, fz), F32),
            jax.ShapeDtypeStruct((flat, sz), F32),
            jax.ShapeDtypeStruct((ni, fy, fz), F32),
        ),
        in_specs=[any_spec] * 11 + [vmem_spec] * 6 + [smem_spec] * 2,
        out_specs=(any_spec,) * 3,
        scratch_shapes=scratch,
        compiler_params=pltpu.CompilerParams(
            collective_id=0, has_side_effects=True, vmem_limit_bytes=60 * 1024 * 1024
        ),
        cost_estimate=pl.CostEstimate(flops=200000000, bytes_accessed=14000000, transcendentals=200000),
    )(
        right_side, storage, trans_x, trans_y, trans_z, sat_logit, porosity,
        background.reshape(flat, sz), wave_prev.reshape(flat, sz), wave_now.reshape(flat, sz),
        data_residual.reshape(flat, sz),
        well_cells.reshape(1, -1), well_rates.reshape(1, -1),
        y_index.reshape(1, -1), y_frac.reshape(1, -1), z_index.reshape(1, -1), z_frac.reshape(1, -1),
        y_index, y_frac,
    )
    results = (pressure, wavefield, sat_gradient)
    pressure, wavefield, sat_gradient = pl.pallas_call(
        move_out,
        out_shape=tuple(jax.ShapeDtypeStruct(r.shape, F32) for r in results),
        in_specs=[any_spec] * 3,
        out_specs=(any_spec,) * 3,
        scratch_shapes=[vm(*r.shape) for r in results] + [dma((3, MOVES)), dma((3, MOVES))],
        compiler_params=pltpu.CompilerParams(vmem_limit_bytes=60 * 1024 * 1024),
    )(*results)
    return pressure, wavefield.reshape(sy, nx, sz), sat_gradient


def solution(mesh):
    cells = P(("grp", "sx"), None, None)
    waves = P(None, ("grp", "sx"), None)
    in_specs = (
        cells, cells, P("grp", None), cells, cells, P("grp"), P("grp"), cells, cells,
        P(), P(), P(), P(), waves, waves, waves, waves,
    )
    return jax.shard_map(
        functools.partial(per_device, mesh.shape["sx"]),
        mesh=mesh, in_specs=in_specs, out_specs=(cells, waves, cells), check_vma=False,
    )
```
